128 devices in a mesh: row: 16 (over y, x), col: 4 (over z), layer: 2 (over core).
Axes of the slice: x: 4, y: 4, z: 4, core: 2. Of those that a mesh axis runs over, the one named last changes fastest.
Arguments:
- left_blocks: float32 [2, 8192, 8192], P('layer', 'row', 'col'), may hold values from -6 to 6
- left_pattern: int32 [2, 64, 64], P('layer', 'row', 'col'), may hold values 0 or 1
- right_blocks: float32 [2, 8192, 4096], P('layer', 'row', 'col'), may hold values from -0.078125 to 0.078125
- right_pattern: int32 [2, 64, 32], P('layer', 'row', 'col'), may hold values 0 or 1
- keep_mask: int32 [16, 4, 32], P('row', 'col'), may hold values 0 or 1
- owner: int32 [16, 4, 32, 1], P('row', 'col'), may hold values from 0 to 1; in each aligned block of 32 rows (0 to 31, 32 to 63, ..., all dimensions but the last counted through in order) at most 32 rows name the same one
Outputs:
- owned: float32 [16, 4, 64, 128, 128], P('row', 'col', 'layer')
The draws below stay inside these ranges and needn't reach their ends.
Inputs may be any that keep to these rules, and one draw needn't show every extreme that they name: An owner may be named by all 32 blocks of a tile, and some tile reaches that, so each owner needs 32 slots.
All inputs are finite; a program needn't handle non-finite values. No bound on the sum of `left_pattern` or of `right_pattern` or of `keep_mask` on one device may be relied on, other than what follows from the above.
Results may differ from the reference program's by a relative error of at most 0.0001.
Values sent between devices are 32-bit elements; how exact they have to be, the bound alone decides.
No kernel may reach another device: no remote copies, remote signals or barrier semaphores. Data moves between devices by JAX's collectives and lax.ppermute only.
A program may use at most 128 MiB of HBM per device.

```python
import math
import jax
import jax.numpy as jnp
import numpy as np
from jax import lax

BS = 128
RB_DEV = 4
CB_DEV = 8
TILE = 32
CAP = 32
KBLK = 64
KW = 8192
KTOT = 16384
RBLK = 64
CBLK = 32
ROWS = 8192
COLS = 4096
N_ROW = 16
N_COL = 4
N_LAYER = 2


def set_ends(drawn, stream_key, least, top_value):
    extent = drawn.shape
    index_at = [jax.random.randint(jax.random.fold_in(stream_key, axis), (), 0, extent[axis]) for axis in range(len(extent))]
    drawn = drawn.at[tuple(index_at)].set(least)
    longest = extent.index(max(extent))
    index_at[longest] = (index_at[longest] + 1) % extent[longest]
    return drawn.at[tuple(index_at)].set(top_value)


def levels(rng, shape, shards, least, top_value):
    factor_of = 1.0
    for axis_at, blocks in shards:
        steps = jax.random.uniform(jax.random.fold_in(jax.random.fold_in(rng, 6), axis_at), (blocks,), jnp.float32, least / len(shards), top_value / len(shards))
        factor_of = factor_of * jnp.repeat(jnp.exp(steps), shape[axis_at] // blocks).reshape((-1,) + (1,) * (len(shape) - 1 - axis_at))
    return factor_of


def assign_block(rng, own, number, rows, amount, top, most, lean):
    sequence = jax.random.permutation(rng, amount)
    crowded, ordinary = shares(amount, rows * top, most, lean, True), shares(amount, rows * top, most, lean, False)
    places = jnp.arange(amount)

    def named(sizes, offset_by):
        used = int((sizes > 0).sum())
        fixed = max(1, used // 4)
        shifted = fixed + (places - fixed + offset_by * (used - fixed)) % max(1, amount - fixed)
        return jnp.zeros((amount,), jnp.int32).at[sequence[jnp.where(places < fixed, places, shifted)]].set(jnp.asarray(sizes, jnp.int32))

    sizes = jnp.where(number % 4 == 0, named(crowded, number // 4), named(ordinary, number - number // 4 - 1))
    mixed = jax.random.permutation(jax.random.fold_in(own, 3), amount)
    source_of, sink = mixed[0:amount // 2 * 2:2], mixed[1:amount // 2 * 2:2]
    room = jnp.minimum(sizes[source_of] - 1, most - sizes[sink]) // 2
    room = jnp.where((source_of == sequence[0]) | (sink == sequence[0]) | (sizes[sink] == 0), 0, jnp.maximum(room, 0))
    shifted = jax.random.randint(jax.random.fold_in(own, 4), (amount // 2,), 0, 1 << 20) % (room + 1)
    sizes = sizes.at[source_of].add(-shifted).at[sink].add(shifted)
    labels = jnp.searchsorted(jnp.cumsum(sizes), jnp.arange(rows * top), side="right").astype(jnp.int32)
    grid = labels.reshape(top, rows).T
    grid = grid[jax.random.permutation(jax.random.fold_in(own, 1), rows)]
    offset_by = jax.random.randint(jax.random.fold_in(own, 2), (rows, 1), 0, top)
    return jnp.take_along_axis(grid, (jnp.arange(top)[None, :] + offset_by) % top, axis=1)


def shares(number_of, total, most, skew, full):
    portions = [(1 << 20) // math.isqrt(grade ** skew) + 1 for grade in range(1, number_of + 1)]
    largest = most if full else min(most, max(-(-total // number_of), total * portions[0] // sum(portions)))
    least = 1 if total - largest >= number_of - 1 else 0
    holding, spare = [largest] + [least] * (number_of - 1), total - largest - least * (number_of - 1)
    while spare > 0:
        free = [i for i in range(1, number_of) if holding[i] < largest] or [i for i in range(1, number_of) if holding[i] < most]
        mass, budget = sum([portions[i] for i in free]), spare
        for i in free:
            extra = min(most - holding[i], max(1, budget * portions[i] // mass), spare)
            holding[i] = holding[i] + extra
            spare = spare - extra
    return np.array(holding)


def gaussian(key, extent, scale, most, cuts=(), kind=jnp.bfloat16):
    result = scale * jax.random.normal(key, extent, jnp.float32)
    if cuts:
        result = result * levels(key, extent, cuts, -0.22, 0.18)
    return jnp.clip(result, -most, most).astype(kind)


def setup_inputs(seed: int = 0) -> dict:
    splits = jax.random.split(jax.random.key(seed), 7)
    left_blocks = gaussian(splits[0], (N_LAYER, ROWS, KW), 1.0, 6.0, ((0, 2), (1, 16), (2, 4)), jnp.float32)
    left_pattern = set_ends((jax.random.randint(splits[1], (N_LAYER, RBLK, KBLK), 0, 3) < 1).astype(jnp.int32), jax.random.fold_in(splits[1], 1), 0, 1)
    right_blocks = gaussian(splits[2], (N_LAYER, KW, COLS), (KTOT // 3) ** -0.5, 0.078125, ((0, 2), (1, 16), (2, 4)), jnp.float32)
    right_pattern = set_ends((jax.random.randint(splits[3], (N_LAYER, KBLK, CBLK), 0, 3) < 1).astype(jnp.int32), jax.random.fold_in(splits[3], 1), 0, 1)
    keep_mask = set_ends((jax.random.randint(splits[4], (N_ROW, N_COL, TILE), 0, 3) < 2).astype(jnp.int32), jax.random.fold_in(splits[4], 1), 0, 1)
    owner_keys = jax.random.split(jax.random.fold_in(splits[5], 1), N_ROW * N_COL * TILE // TILE)
    owner_turns = jax.random.permutation(jax.random.fold_in(splits[5], 3), N_ROW * N_COL * TILE // TILE)
    owner = jax.vmap(lambda own, number: assign_block(jax.random.fold_in(splits[5], 2), own, number, TILE, N_LAYER, 1, CAP, 2))(owner_keys, owner_turns).reshape((N_ROW, N_COL, TILE, 1))
    return dict(left_blocks=left_blocks, left_pattern=left_pattern, right_blocks=right_blocks, right_pattern=right_pattern, keep_mask=keep_mask, owner=owner)


def spread(pattern):
    wide = jnp.repeat(jnp.repeat(pattern, BS, axis=0), BS, axis=1)
    return wide.astype(jnp.float32)


def reference(left_blocks, left_pattern, right_blocks, right_pattern, keep_mask, owner):
    def add_slab(total, slab):
        left_one, left_pat, right_one, right_pat = slab
        left_eff = left_one * spread(left_pat)
        right_eff = right_one * spread(right_pat)
        return total + jnp.dot(left_eff, right_eff, preferred_element_type=jnp.float32, precision=lax.Precision.HIGHEST), None

    start = jnp.zeros((ROWS, COLS), jnp.float32)
    product, unused = lax.scan(add_slab, start, (left_blocks, left_pattern, right_blocks, right_pattern))
    tiles = product.reshape(N_ROW, RB_DEV, BS, N_COL, CB_DEV, BS).transpose(0, 3, 1, 4, 2, 5)
    tiles = tiles.reshape(N_ROW, N_COL, TILE, BS, BS)
    tiles = tiles * keep_mask.astype(jnp.float32)[..., None, None]
    owners = owner[..., 0]
    onehot = (owners[..., None] == jnp.arange(N_LAYER, dtype=jnp.int32)).astype(jnp.int32)
    before = jnp.cumsum(onehot, axis=2) - onehot
    rank = jnp.sum(before * onehot, axis=-1)
    slot = owners * CAP + rank
    place = (slot[..., None, :] == jnp.arange(N_LAYER * CAP, dtype=jnp.int32)[:, None]).astype(jnp.float32)
    return jnp.einsum("ijst,ijtab->ijsab", place, tiles, precision=lax.Precision.HIGHEST)
```

```python
import functools

import jax
import jax.numpy as jnp
from jax import lax
from jax.experimental import pallas as pl
from jax.experimental.pallas import tpu as pltpu
from jax.sharding import PartitionSpec as P

BS = 128
HDR = 8
COUNT = 127
FLAG = 126
L_CAP = 36
R_HALF = 11
G_A = 16
G_B = 16
G_CAP = G_A + G_B
AXES = ("row", "col", "layer")
F32 = jnp.float32
BF16 = jnp.bfloat16


def dense(left_blocks, left_pattern, right_blocks, right_pattern, keep_mask, owner):
    def spread(pattern):
        wide = jnp.repeat(jnp.repeat(pattern, BS, axis=0), BS, axis=1)
        return wide.astype(F32)

    left_eff = left_blocks[0] * spread(left_pattern[0])
    right_eff = right_blocks[0] * spread(right_pattern[0])
    row_blocks = left_pattern.shape[1]
    col_blocks = right_pattern.shape[2]
    right_all = lax.all_gather(right_eff, "row", axis=0, tiled=True)
    partial_sum = jnp.dot(
        lax.all_gather(left_eff, "col", axis=1, tiled=True),
        right_all,
        preferred_element_type=F32,
        precision=lax.Precision.HIGHEST,
    )
    tile_count = row_blocks * col_blocks
    tiles = (
        partial_sum.reshape(row_blocks, BS, col_blocks, BS)
        .transpose(0, 2, 1, 3)
        .reshape(tile_count, BS, BS)
    )
    tiles = tiles * keep_mask[0, 0].astype(F32)[:, None, None]
    other = lax.ppermute(tiles, "layer", [(0, 1), (1, 0)])
    tiles = tiles + other
    owners = owner[0, 0, :, 0]
    onehot = (owners[:, None] == jnp.arange(2, dtype=jnp.int32)[None, :]).astype(jnp.int32)
    before = jnp.cumsum(onehot, axis=0) - onehot
    rank = jnp.sum(before * onehot, axis=1)
    slot = owners * tile_count + rank
    wanted = lax.axis_index("layer") * tile_count + jnp.arange(tile_count, dtype=jnp.int32)
    pick = (slot[None, :] == wanted[:, None]).astype(F32)
    return jnp.einsum("st,tab->sab", pick, tiles, precision=lax.Precision.HIGHEST)


def ring(array, axis):
    pairs = []
    for y in range(4):
        for x in range(4):
            for z in range(4):
                for core in range(2):
                    to = {"y": y, "x": x, "z": z}
                    to[axis] = (to[axis] + 1 - 2 * core) % 4
                    source = ((y * 4 + x) * 4 + z) * 2 + core
                    target = ((to["y"] * 4 + to["x"]) * 4 + to["z"]) * 2 + core
                    pairs.append((source, target))
    return lax.ppermute(array, AXES, pairs)


def hops(array, axis):
    out = [array]
    for _ in range(3):
        out.append(ring(out[-1], axis))
    return out


def block_rows(slot, head=HDR):
    return pl.ds(pl.multiple_of(head + slot * BS, 8), BS)


def blank():
    return jnp.zeros((HDR, BS), F32)


def place(header, lane, value):
    lanes = lax.broadcasted_iota(jnp.int32, (HDR, BS), 1)
    return jnp.where(lanes == lane, value, header)


def pack_right_kernel(lpat, rpat, right, a_out, b_out, codes, head, sems, hsems):
    row = lax.axis_index("row")
    flip = row & 1

    def scan(i, n):
        codes[n] = i
        return n + rpat[0, i >> 3, i & 7]

    n = lax.fori_loop(0, 32, scan, jnp.int32(0))
    n_left = lax.fori_loop(0, 64, lambda i, s: s + lpat[0, i >> 4, i & 15], jnp.int32(0))
    over = (n > 2 * R_HALF) | (n_left > L_CAP)
    m = jnp.minimum(n, 2 * R_HALF)

    def copies(s):
        code = codes[s]
        source = right.at[0, pl.ds(pl.multiple_of((code >> 3) * BS, BS), BS), pl.ds(pl.multiple_of((code & 7) * BS, BS), BS)]
        rows = block_rows(s >> 1)
        return (
            pltpu.make_async_copy(source, a_out.at[rows], sems.at[s]),
            pltpu.make_async_copy(source, b_out.at[rows], sems.at[s]),
        )

    def start(s, headers):
        in_a = ((s + flip) & 1) == 0
        to_a, to_b = copies(s)

        @pl.when(in_a)
        def _():
            to_a.start()

        @pl.when(jnp.logical_not(in_a))
        def _():
            to_b.start()

        code = (row * 32 + codes[s]).astype(F32)
        slot = s >> 1
        return (
            place(headers[0], jnp.where(in_a, slot, -1), code),
            place(headers[1], jnp.where(in_a, -1, slot), code),
        )

    header_a, header_b = lax.fori_loop(0, m, start, (blank(), blank()))
    count_a = (m + 1 - flip) >> 1
    flag = over.astype(F32)
    head[0] = place(place(header_a, COUNT, count_a.astype(F32)), FLAG, flag)
    head[1] = place(place(header_b, COUNT, (m - count_a).astype(F32)), FLAG, flag)
    ha = pltpu.make_async_copy(head.at[0], a_out.at[pl.ds(0, HDR)], hsems.at[0])
    hb = pltpu.make_async_copy(head.at[1], b_out.at[pl.ds(0, HDR)], hsems.at[1])
    ha.start()
    hb.start()

    def finish(s, _):
        copies(s)[0].wait()
        return 0

    lax.fori_loop(0, m, finish, 0)
    ha.wait()
    hb.wait()


def pack_left_kernel(lpat, left, out, codes, head, sems, hsem):
    base = lax.axis_index("col") * 64

    def scan(i, n):
        codes[n] = i
        return n + lpat[0, i & 3, i >> 2]

    n = lax.fori_loop(0, 64, scan, jnp.int32(0))
    m = jnp.minimum(n, L_CAP)

    def copy(s):
        code = codes[s]
        source = left.at[0, pl.ds(pl.multiple_of((code & 3) * BS, BS), BS), pl.ds(pl.multiple_of((code >> 2) * BS, BS), BS)]
        return pltpu.make_async_copy(source, out.at[block_rows(s)], sems.at[s])

    def start(s, header):
        copy(s).start()
        return place(header, s, (base + codes[s]).astype(F32))

    header = lax.fori_loop(0, m, start, blank())
    head[...] = place(header, COUNT, m.astype(F32))
    h = pltpu.make_async_copy(head, out.at[pl.ds(0, HDR)], hsem)
    h.start()

    def finish(s, _):
        copy(s).wait()
        return 0

    lax.fori_loop(0, m, finish, 0)
    h.wait()


def merge_kernel(*refs):
    ins = (refs[0:4], refs[4:8])
    outs = (refs[8:10], refs[10:12])
    seen, head, sems, hsems = refs[12:]
    reads = []
    for half in range(2):
        for i in range(4):
            read = pltpu.make_async_copy(ins[half][i].at[pl.ds(0, HDR)], seen.at[half, i], hsems.at[half * 4 + i])
            read.start()
            reads.append(read)
    for read in reads:
        read.wait()
    totals = []
    for half in range(2):
        first, second = outs[half]
        header = blank()
        total = jnp.int32(0)
        flag = F32(0) if False else jnp.float32(0)
        for i in range(4):
            count = seen[half, i, 0, COUNT].astype(jnp.int32)
            flag = jnp.maximum(flag, seen[half, i, 0, FLAG])

            def start(s, header, half=half, i=i, total=total, first=first, second=second):
                g = total + s
                source = ins[half][i].at[block_rows(s)]

                @pl.when(g < G_A)
                def _():
                    pltpu.make_async_copy(source, first.at[block_rows(g)], sems.at[half, g]).start()

                @pl.when((g >= G_A) & (g < G_CAP))
                def _():
                    pltpu.make_async_copy(source, second.at[block_rows(g - G_A, 0)], sems.at[half, g]).start()

                return place(header, jnp.where(g < G_CAP, g, -1), seen[half, i, 0, s])

            header = lax.fori_loop(0, count, start, header)
            total = total + count
        kept = jnp.minimum(total, G_CAP)
        flag = jnp.where(total > G_CAP, jnp.float32(1), flag)
        head[half] = place(place(header, COUNT, kept.astype(F32)), FLAG, flag)
        pltpu.make_async_copy(head.at[half], first.at[pl.ds(0, HDR)], hsems.at[8 + half]).start()
        totals.append(kept)
    for half in range(2):
        first, second = outs[half]

        def finish(s, _, half=half, first=first):
            pltpu.make_async_copy(ins[half][0].at[block_rows(0)], first.at[block_rows(0)], sems.at[half, s]).wait()
            return 0

        lax.fori_loop(0, totals[half], finish, 0)
        pltpu.make_async_copy(head.at[half], first.at[pl.ds(0, HDR)], hsems.at[8 + half]).wait()


def split(block):
    high = block.astype(BF16)
    low = (block - high.astype(F32)).astype(BF16)
    return jnp.concatenate([high, low], axis=1)


def multiply_kernel(groups, begin, final, *refs):
    refs = list(refs)
    lefts = refs[:4]
    del refs[:4]
    parts = []
    for first, second in groups:
        parts.append((refs.pop(0), refs.pop(0) if second else None))
    acc_in = None if begin else refs.pop(0)
    if final:
        keep_ref, owner_ref = refs.pop(0), refs.pop(0)
        mine_ref, send_ref, flag_ref = refs.pop(0), refs.pop(0), refs.pop(0)
        acc = refs.pop(0)
    else:
        acc = refs.pop(0)
    lv, rv, lhead, rhead, table, work, lsems, rsems, asem, hsems = refs
    heads = []
    for i in range(4):
        heads.append(pltpu.make_async_copy(lefts[i].at[pl.ds(0, HDR)], lhead.at[i], hsems.at[i]))
    for g, (first, _) in enumerate(parts):
        heads.append(pltpu.make_async_copy(first.at[pl.ds(0, HDR)], rhead.at[g], hsems.at[4 + g]))
    for copy in heads:
        copy.start()
    loads = []
    for i in range(4):
        loads.append(pltpu.make_async_copy(lefts[i].at[pl.ds(HDR, L_CAP * BS)], lv.at[pl.ds(i * L_CAP * BS, L_CAP * BS)], lsems.at[i]))
    for g, (first, second) in enumerate(parts):
        if groups[g][0]:
            loads.append(pltpu.make_async_copy(first.at[pl.ds(HDR, G_A * BS)], rv.at[pl.ds(g * G_CAP * BS, G_A * BS)], rsems.at[2 * g]))
        if second is not None:
            loads.append(pltpu.make_async_copy(second, rv.at[pl.ds((g * G_CAP + G_A) * BS, G_B * BS)], rsems.at[2 * g + 1]))
    for copy in loads:
        copy.start()
    if begin:
        acc[...] = jnp.zeros(acc.shape, F32)
    else:
        acc_load = pltpu.make_async_copy(acc_in, acc, asem)
        acc_load.start()
    zero_slot = 4 * L_CAP
    lv[pl.ds(zero_slot * BS, BS)] = jnp.zeros((BS, BS), F32)

    def clear(i, _):
        table[i] = zero_slot
        return 0

    lax.fori_loop(0, 256, clear, 0)
    for copy in heads:
        copy.wait()
    for i in range(4):

        def note(s, _, i=i):
            table[lhead[i, 0, s].astype(jnp.int32)] = i * L_CAP + s
            return 0

        lax.fori_loop(0, lhead[i, 0, COUNT].astype(jnp.int32), note, 0)
    items = jnp.int32(0)
    for g in range(len(parts)):
        count = rhead[g, 0, COUNT].astype(jnp.int32)
        low = 0 if groups[g][0] else G_A
        high = count if groups[g][1] else jnp.minimum(count, G_A)

        def note(s, n, g=g):
            work[n] = rhead[g, 0, s].astype(jnp.int32) * 256 + g * G_CAP + s
            return n + 1

        items = lax.fori_loop(low, high, note, items)
    for copy in loads:
        copy.wait()
    if not begin:
        acc_load.wait()

    def step(w, _):
        entry = work[w]
        code = lax.shift_right_logical(entry, 8)
        source = entry & 255
        k4 = lax.shift_right_logical(code, 3) * 4
        c = code & 7
        right = split(rv[pl.ds(pl.multiple_of(source * BS, BS), BS)])
        weights = jnp.concatenate([right, right], axis=0)
        rows = [split(lv[pl.ds(pl.multiple_of(table[k4 + r] * BS, BS), BS)]) for r in range(4)]
        result = jnp.dot(jnp.concatenate(rows, axis=0), weights, preferred_element_type=F32)
        acc[c] += result[:, :BS] + result[:, BS:]
        return 0

    lax.fori_loop(0, items, step, 0)

    if final:
        me = lax.axis_index("layer")
        mine_ref[...] = jnp.zeros(mine_ref.shape, F32)
        send_ref[...] = jnp.zeros(send_ref.shape, F32)
        counts = [jnp.int32(0), jnp.int32(0)]
        for t in range(32):
            who = owner_ref[0, 0, t]
            slot = jnp.where(who == 0, counts[0], counts[1])
            block = acc[t % 8, pl.ds((t // 8) * BS, BS)] * keep_ref[0, 0, t].astype(F32)

            @pl.when(who == me)
            def _(block=block, slot=slot):
                mine_ref[slot] = block

            @pl.when(who != me)
            def _(block=block, slot=slot):
                send_ref[slot] = block

            counts[0] = counts[0] + (who == 0).astype(jnp.int32)
            counts[1] = counts[1] + (who != 0).astype(jnp.int32)
        flag = jnp.float32(0)
        for g in range(len(parts)):
            flag = jnp.maximum(flag, rhead[g, 0, FLAG])
        flag_ref[...] = jnp.full((HDR, BS), flag)


ANY = pl.BlockSpec(memory_space=pl.ANY)
SMEM = pl.BlockSpec(memory_space=pltpu.SMEM)
VMEM = pl.BlockSpec(memory_space=pltpu.VMEM)
PARAMS = pltpu.CompilerParams(vmem_limit_bytes=40 * 2**20)


def packed(blocks, head=HDR):
    return jax.ShapeDtypeStruct((head + blocks * BS, BS), F32)


def multiply(lefts, groups, parts, acc, keep=None, owner=None):
    begin, final = acc is None, keep is not None
    operands = list(lefts)
    specs = [ANY] * 4
    for (first, second), (one, two) in zip(groups, parts):
        operands.append(one)
        specs.append(ANY)
        if second:
            operands.append(two)
            specs.append(ANY)
    if not begin:
        operands.append(acc)
        specs.append(ANY)
    tile = (8, 4 * BS, BS)
    scratch = []
    if final:
        operands += [keep, owner]
        specs += [SMEM, SMEM]
        out_shape = [jax.ShapeDtypeStruct((32, BS, BS), F32)] * 2 + [jax.ShapeDtypeStruct((HDR, BS), F32)]
        out_specs = [VMEM] * 3
        scratch.append(pltpu.VMEM(tile, F32))
    else:
        out_shape = jax.ShapeDtypeStruct(tile, F32)
        out_specs = VMEM
    number = len(groups)
    scratch += [
        pltpu.VMEM(((4 * L_CAP + 1) * BS, BS), F32),
        pltpu.VMEM((number * G_CAP * BS, BS), F32),
        pltpu.SMEM((4, HDR, BS), F32),
        pltpu.SMEM((number, HDR, BS), F32),
        pltpu.SMEM((256,), jnp.int32),
        pltpu.SMEM((number * G_CAP,), jnp.int32),
        pltpu.SemaphoreType.DMA((4,)),
        pltpu.SemaphoreType.DMA((2 * number,)),
        pltpu.SemaphoreType.DMA,
        pltpu.SemaphoreType.DMA((4 + number,)),
    ]
    work = 12 * number
    return pl.pallas_call(
        functools.partial(multiply_kernel, groups, begin, final),
        out_shape=out_shape,
        in_specs=specs,
        out_specs=out_specs,
        scratch_shapes=scratch,
        compiler_params=PARAMS,
        cost_estimate=pl.CostEstimate(flops=work * 4 * 2 * 512 * BS * BS, bytes_accessed=16 * 2**20, transcendentals=0),
    )(*operands)


def local(left_blocks, left_pattern, right_blocks, right_pattern, keep_mask, owner):
    a0, b0 = pl.pallas_call(
        pack_right_kernel,
        out_shape=[packed(R_HALF)] * 2,
        in_specs=[SMEM, SMEM, ANY],
        out_specs=[ANY, ANY],
        scratch_shapes=[
            pltpu.SMEM((33,), jnp.int32),
            pltpu.VMEM((2, HDR, BS), F32),
            pltpu.SemaphoreType.DMA((2 * R_HALF,)),
            pltpu.SemaphoreType.DMA((2,)),
        ],
        compiler_params=PARAMS,
    )(left_pattern, right_pattern, right_blocks)
    l0 = pl.pallas_call(
        pack_left_kernel,
        out_shape=packed(L_CAP),
        in_specs=[SMEM, ANY],
        out_specs=ANY,
        scratch_shapes=[
            pltpu.SMEM((65,), jnp.int32),
            pltpu.VMEM((HDR, BS), F32),
            pltpu.SemaphoreType.DMA((L_CAP,)),
            pltpu.SemaphoreType.DMA,
        ],
        compiler_params=PARAMS,
    )(left_pattern, left_blocks)
    halves_a = hops(a0, "x")
    halves_b = hops(b0, "y")
    lefts = hops(l0, "z")
    merged = pl.pallas_call(
        merge_kernel,
        out_shape=[packed(G_A), packed(G_B, 0)] * 2,
        in_specs=[ANY] * 8,
        out_specs=[ANY] * 4,
        scratch_shapes=[
            pltpu.SMEM((2, 4, HDR, BS), F32),
            pltpu.VMEM((2, HDR, BS), F32),
            pltpu.SemaphoreType.DMA((2, G_CAP)),
            pltpu.SemaphoreType.DMA((10,)),
        ],
        compiler_params=PARAMS,
    )(*halves_a, *halves_b)
    ga = list(zip(hops(merged[0], "y"), hops(merged[1], "y")))
    gb = list(zip(hops(merged[2], "x"), hops(merged[3], "x")))
    both = (True, True)
    acc = multiply(lefts, [both] * 6, [ga[0], gb[0], ga[1], gb[1], ga[2], gb[2]], None)
    mine, send, flag = multiply(lefts, [both] * 2, [ga[3], gb[3]], acc, keep_mask, owner.reshape(1, 1, 32))
    heads = [g[0][:1, FLAG] for g in ga + gb]
    flag = functools.reduce(jnp.maximum, heads)
    for _ in range(3):
        flag = jnp.maximum(flag, ring(flag, "z"))
    flag = jnp.maximum(flag, lax.ppermute(flag, "layer", [(0, 1), (1, 0)]))
    other = lax.ppermute(send, "layer", [(0, 1), (1, 0)])
    owned = lax.cond(
        flag[0] > 0,
        lambda: dense(left_blocks, left_pattern, right_blocks, right_pattern, keep_mask, owner),
        lambda: mine + other,
    )
    return owned[None, None]


def solution(mesh):
    return jax.shard_map(
        local,
        mesh=mesh,
        in_specs=(
            P("layer", "row", "col"),
            P("layer", "row", "col"),
            P("layer", "row", "col"),
            P("layer", "row", "col"),
            P("row", "col", None),
            P("row", "col", None, None),
        ),
        out_specs=P("row", "col", "layer", None, None),
        check_vma=False,
    )
```

```python
import functools

import jax
import jax.numpy as jnp
from jax import lax
from jax.experimental import pallas as pl
from jax.experimental.pallas import tpu as pltpu
from jax.sharding import PartitionSpec as P

BS = 128
HDR = 8
COUNT = 127
FLAG = 126
L_CAP = 36
R_PART = 6
R_HALF = 2 * R_PART
PARCEL = HDR + R_PART * BS
G_LATE = 4
HEADS = 4 * HDR
GROUP = HEADS + (2 * R_PART + G_LATE) * BS
MERGE_COST = 70
UNROLL = 8
AXES = ("row", "col", "layer")
F32 = jnp.float32
BF16 = jnp.bfloat16


def dense(left_blocks, left_pattern, right_blocks, right_pattern, keep_mask, owner):
    def spread(pattern):
        wide = jnp.repeat(jnp.repeat(pattern, BS, axis=0), BS, axis=1)
        return wide.astype(F32)

    left_eff = left_blocks[0] * spread(left_pattern[0])
    right_eff = right_blocks[0] * spread(right_pattern[0])
    row, col = lax.axis_index("row"), lax.axis_index("col")
    way = 1 - 2 * lax.axis_index("layer")
    left_all = jnp.zeros((4 * BS, 64 * BS), F32)
    for step, part in enumerate(hops(left_eff, "z")):
        start = ((col - step * way) & 3) * (16 * BS)
        left_all = lax.dynamic_update_slice(left_all, part, (0, start))
    total = jnp.zeros((4 * BS, 8 * BS), F32)
    for step_x, along_x in enumerate(hops(right_eff, "x")):
        for step_y, part in enumerate(hops(along_x, "y")):
            origin = (((row >> 2) - step_y * way) & 3) * 4 + (((row & 3) - step_x * way) & 3)
            columns = lax.dynamic_slice(left_all, (0, origin * (4 * BS)), (4 * BS, 4 * BS))
            total = total + jnp.dot(columns, part, preferred_element_type=F32, precision=lax.Precision.HIGHEST)
    tiles = total.reshape(4, BS, 8, BS).transpose(0, 2, 1, 3).reshape(32, BS, BS)
    tiles = tiles * keep_mask[0, 0].astype(F32)[:, None, None]
    tiles = tiles + swap(tiles)
    owners = owner[0, 0, :, 0]
    onehot = (owners[:, None] == jnp.arange(2, dtype=jnp.int32)[None, :]).astype(jnp.int32)
    before = jnp.cumsum(onehot, axis=0) - onehot
    slot = owners * 32 + jnp.sum(before * onehot, axis=1)
    wanted = lax.axis_index("layer") * 32 + jnp.arange(32, dtype=jnp.int32)
    pick = (slot[None, :] == wanted[:, None]).astype(F32)
    return jnp.einsum("st,tab->sab", pick, tiles, precision=lax.Precision.HIGHEST)


def swap(array):
    return lax.ppermute(array, "layer", [(0, 1), (1, 0)])


def ring(array, axis, distance=1):
    pairs = []
    for y in range(4):
        for x in range(4):
            for z in range(4):
                for core in range(2):
                    to = {"y": y, "x": x, "z": z}
                    to[axis] = (to[axis] + distance * (1 - 2 * core)) % 4
                    source = ((y * 4 + x) * 4 + z) * 2 + core
                    target = ((to["y"] * 4 + to["x"]) * 4 + to["z"]) * 2 + core
                    pairs.append((source, target))
    return lax.ppermute(array, AXES, pairs)


def hops(array, axis, number=3):
    out = [array]
    for _ in range(number):
        out.append(ring(out[-1], axis))
    return out


def block_rows(slot, head=HDR):
    return pl.ds(pl.multiple_of(head + slot * BS, 8), BS)


def blank():
    return jnp.zeros((HDR, BS), F32)


def place(header, lane, value):
    lanes = lax.broadcasted_iota(jnp.int32, (HDR, BS), 1)
    return jnp.where(lanes == lane, value, header)


def pack_kernel(lpat, rpat, left, right, a_early, b_early, a_late, b_late, l_out, codes, lcodes, head, lhead, sems, lsems, hsems):
    row = lax.axis_index("row")
    flip = row & 1
    base = lax.axis_index("col") * 64

    def scan(i, n):
        codes[n] = i
        return n + rpat[0, i >> 3, i & 7]

    n = lax.fori_loop(0, 32, scan, jnp.int32(0))
    m = jnp.minimum(n, 2 * R_HALF)

    def start(s, headers):
        in_a = ((s + flip) & 1) == 0
        code = codes[s]
        slot = s >> 1
        source = right.at[0, pl.ds(pl.multiple_of((code >> 3) * BS, BS), BS), pl.ds(pl.multiple_of((code & 7) * BS, BS), BS)]
        which = jnp.where(in_a, 0, 1) + jnp.where(slot < R_PART, 0, 2)
        rows = block_rows(jnp.where(slot < R_PART, slot, slot - R_PART))
        for i, out in enumerate((a_early, b_early, a_late, b_late)):

            @pl.when(which == i)
            def _(out=out):
                pltpu.make_async_copy(source, out.at[rows], sems.at[s]).start()

        value = (row * 32 + code).astype(F32)
        return (
            place(headers[0], jnp.where(in_a, slot, -1), value),
            place(headers[1], jnp.where(in_a, -1, slot), value),
        )

    header_a, header_b = lax.fori_loop(0, m, start, (blank(), blank()))

    def scan_left(i, n):
        lcodes[n] = i
        return n + lpat[0, i & 3, i >> 2]

    n_left = lax.fori_loop(0, 64, scan_left, jnp.int32(0))
    m_left = jnp.minimum(n_left, L_CAP)

    def start_left(s, header):
        code = lcodes[s]
        source = left.at[0, pl.ds(pl.multiple_of((code & 3) * BS, BS), BS), pl.ds(pl.multiple_of((code >> 2) * BS, BS), BS)]
        pltpu.make_async_copy(source, l_out.at[block_rows(s)], lsems.at[s]).start()
        return place(header, s, (base + code).astype(F32))

    header_l = lax.fori_loop(0, m_left, start_left, blank())
    flag = ((n > 2 * R_HALF) | (n_left > L_CAP)).astype(F32)
    count_a = (m + 1 - flip) >> 1
    head[0] = place(place(header_a, COUNT, count_a.astype(F32)), FLAG, flag)
    head[1] = place(place(header_b, COUNT, (m - count_a).astype(F32)), FLAG, flag)
    lhead[...] = place(header_l, COUNT, m_left.astype(F32))
    copies = [
        pltpu.make_async_copy(head.at[0], a_early.at[pl.ds(0, HDR)], hsems.at[0]),
        pltpu.make_async_copy(head.at[1], b_early.at[pl.ds(0, HDR)], hsems.at[1]),
        pltpu.make_async_copy(lhead, l_out.at[pl.ds(0, HDR)], hsems.at[2]),
    ]
    for copy in copies:
        copy.start()

    def finish(s, _):
        pltpu.make_async_copy(right.at[0, pl.ds(0, BS), pl.ds(0, BS)], a_early.at[block_rows(0)], sems.at[s]).wait()
        return 0

    def finish_left(s, _):
        pltpu.make_async_copy(left.at[0, pl.ds(0, BS), pl.ds(0, BS)], l_out.at[block_rows(0)], lsems.at[s]).wait()
        return 0

    lax.fori_loop(0, m, finish, 0)
    lax.fori_loop(0, m_left, finish_left, 0)
    for copy in copies:
        copy.wait()


def merge_kernel(*refs):
    early, late = (refs[0:4], refs[4:8]), (refs[8:12], refs[12:16])
    outs = (refs[16:18], refs[18:20])
    seen, sems, lsems, hsems = refs[20:]
    reads = []
    copies = []
    for half in range(2):
        for i in range(4):
            head = early[half][i].at[pl.ds(0, HDR)]
            reads.append(pltpu.make_async_copy(head, seen.at[half, i], hsems.at[half * 8 + i]))
            reads[-1].start()
            copies.append(pltpu.make_async_copy(head, outs[half][0].at[pl.ds(i * HDR, HDR)], hsems.at[half * 8 + 4 + i]))
            rows = pl.ds(HEADS + (i % 2) * R_PART * BS, R_PART * BS)
            source = early[half][i].at[pl.ds(HDR, R_PART * BS)]
            copies.append(pltpu.make_async_copy(source, outs[half][i // 2].at[rows], sems.at[half * 4 + i]))
    for copy in copies:
        copy.start()
    for read in reads:
        read.wait()
    totals = []
    for half in range(2):
        total = jnp.int32(0)
        for i in range(4):
            count = seen[half, i, 0, COUNT].astype(jnp.int32)

            def start(s, g, half=half, i=i):
                source = late[half][i].at[block_rows(s - R_PART)]
                for j in range(2):

                    @pl.when((g >= j * G_LATE) & (g < (j + 1) * G_LATE))
                    def _(j=j):
                        rows = block_rows(2 * R_PART + g - j * G_LATE, HEADS)
                        pltpu.make_async_copy(source, outs[half][j].at[rows], lsems.at[half, g]).start()

                return g + 1

            total = lax.fori_loop(R_PART, count, start, total)
        totals.append(jnp.minimum(total, 2 * G_LATE))
    for half in range(2):

        def finish(s, _, half=half):
            pltpu.make_async_copy(late[half][0].at[block_rows(0)], outs[half][0].at[block_rows(0, HEADS)], lsems.at[half, s]).wait()
            return 0

        lax.fori_loop(0, totals[half], finish, 0)
    for copy in copies:
        copy.wait()


def flag_kernel(*refs):
    groups, out, heads, sems = refs[0:8], refs[9], refs[10], refs[11]
    copies = []
    for g in range(8):
        copies.append(pltpu.make_async_copy(groups[g].at[pl.ds(0, HEADS)], heads.at[g], sems.at[g]))
        copies[-1].start()
    for copy in copies:
        copy.wait()
    worst = blank()
    most = blank()
    for g in range(8):
        late = blank()
        for i in range(4):
            header = heads[g, i * HDR : (i + 1) * HDR]
            worst = jnp.maximum(worst, header)
            late = late + jnp.maximum(header - R_PART, 0.0)
        most = jnp.maximum(most, late)
    first = lax.broadcasted_iota(jnp.int32, (HDR, BS), 0) == 0
    lanes = lax.broadcasted_iota(jnp.int32, (HDR, BS), 1)
    over = first & (((lanes == FLAG) & (worst > 0.5)) | ((lanes == COUNT) & (most > 2 * G_LATE + 0.5)))
    out[...] = jnp.full((HDR, BS), jnp.max(jnp.where(over, 1.0, 0.0)))


def split(block):
    high = block.astype(BF16)
    low = (block - high.astype(F32)).astype(BF16)
    return jnp.concatenate([high, low], axis=1)


def hold_kernel(step, *refs):
    packed_ref, held, sem = refs[0], refs[-2], refs[-1]
    rows = pl.ds(step * L_CAP * BS, L_CAP * BS)
    copy = pltpu.make_async_copy(packed_ref.at[pl.ds(HDR, L_CAP * BS)], held.at[rows], sem)
    copy.start()
    if step == 0:
        held[pl.ds(4 * L_CAP * BS, BS)] = jnp.zeros((BS, BS), F32)
    copy.wait()


def hold(packed_left, step, held=None, after=()):
    shape = jax.ShapeDtypeStruct(((4 * L_CAP + 1) * BS, BS), F32)
    return pl.pallas_call(
        functools.partial(hold_kernel, step),
        out_shape=shape,
        in_specs=[HBM] + ([] if held is None else [VMEM]) + [ANY] * len(after),
        out_specs=VMEM,
        input_output_aliases={} if held is None else {1: 0},
        scratch_shapes=[pltpu.SemaphoreType.DMA],
        compiler_params=params(1),
    )(packed_left, *([] if held is None else [held]), *after)


def multiply_kernel(n_left, lows, halves, begin, final, *refs):
    refs = list(refs)
    number = len(lows)
    keep, lv = refs.pop(0), refs.pop(0)
    lefts = [refs.pop(0) for _ in range(n_left)]
    parts = [[refs.pop(0) if j == 0 or j in halves else None for j in range(2)] for _ in range(number)]
    if not begin:
        refs.pop(0)
    if final:
        owner, flag_in = refs.pop(0), refs.pop(0)
    acc = refs.pop(0)
    if final:
        mine, send = refs.pop(0), refs.pop(0)
    rv, lhead, rhead, table, work, rsems, hsems = refs
    heads = []
    for i in range(n_left):
        heads.append(pltpu.make_async_copy(lefts[i].at[pl.ds(0, HDR)], lhead.at[i], hsems.at[i]))
    for g in range(number):
        for i in range(4):
            heads.append(pltpu.make_async_copy(parts[g][0].at[pl.ds(i * HDR, HDR)], rhead.at[g, i], hsems.at[4 + g * 4 + i]))
    for copy in heads:
        copy.start()
    loads = []
    for g in range(number):
        for n, j in enumerate(halves):
            rows = pl.ds((g * len(halves) + n) * GROUP, GROUP)
            loads.append(pltpu.make_async_copy(parts[g][j], rv.at[rows], rsems.at[g * len(halves) + n]))
    for copy in loads:
        copy.start()
    if begin:
        acc[...] = jnp.zeros(acc.shape, F32)
    no_left, no_right = 4 * L_CAP, number * len(halves) * GROUP
    rv[pl.ds(no_right, BS)] = jnp.zeros((BS, BS), F32)

    def clear(i, _):
        for j in range(8):
            table[i * 8 + j] = no_left
        return 0

    lax.fori_loop(0, 32, clear, 0)
    for copy in heads:
        copy.wait()
    for i in range(n_left):

        def enter(s, _, i=i):
            table[lhead[i, 0, s].astype(jnp.int32)] = i * L_CAP + s
            return 0

        lax.fori_loop(0, lhead[i, 0, COUNT].astype(jnp.int32), enter, 0)
    pairs = jnp.int32(0)

    def note(code, at, n, low):
        k4 = (code >> 3) * 4
        c = code & 7
        for r in range(4):
            slot = table[k4 + r]
            work[n] = (slot << 20) | (at << 5) | (r * 8 + c)
            n = n + jnp.where((slot >= low * L_CAP) & (slot < no_left), keep[0, 0, r * 8 + c], 0)
        return n

    for g in range(number):
        late = jnp.int32(0)
        for i in range(4):
            count = rhead[g, i, 0, COUNT].astype(jnp.int32)
            if i // 2 in halves:
                first = ((g * len(halves) + halves.index(i // 2)) * GROUP + HEADS + (i % 2) * R_PART * BS) // 8

                def early_one(s, n, g=g, i=i, first=first):
                    return note(rhead[g, i, 0, s].astype(jnp.int32), first + s * (BS // 8), n, lows[g])

                pairs = lax.fori_loop(0, jnp.minimum(count, R_PART), early_one, pairs)
            low = min(halves) * G_LATE
            first = (g * len(halves) * GROUP + HEADS + 2 * R_PART * BS) // 8

            def late_one(s, state, g=g, i=i, low=low, first=first):
                n, at = state
                place_of = jnp.clip(at - low, 0, len(halves) * G_LATE - 1)
                place_of = first + (place_of // G_LATE) * (GROUP // 8) + (place_of % G_LATE) * (BS // 8)
                after = note(rhead[g, i, 0, s].astype(jnp.int32), place_of, n, lows[g])
                inside = (at >= low) & (at < low + len(halves) * G_LATE)
                return jnp.where(inside, after, n), at + 1

            pairs, late = lax.fori_loop(R_PART, count, late_one, (pairs, late))
    for j in range(UNROLL):
        work[pairs + j] = (no_left << 20) | (no_right // 8 << 5)

    for copy in loads:
        copy.wait()

    def step(w, _):
        results = []
        for j in range(UNROLL):
            entry = work[w * UNROLL + j]
            left = split(lv[block_rows(entry >> 20, 0)])
            right = split(rv[pl.ds(pl.multiple_of(((entry >> 5) & 32767) * 8, 8), BS)])
            result = jnp.dot(left, jnp.concatenate([right, right], axis=0), preferred_element_type=F32)
            results.append((entry & 31, result[:, :BS] + result[:, BS:]))
        for tile, result in results:
            acc[tile] += result
        return 0

    lax.fori_loop(0, (pairs + UNROLL - 1) // UNROLL, step, 0)

    if final:
        me = lax.axis_index("layer")
        mine[...] = jnp.zeros(mine.shape, F32)
        send[...] = jnp.zeros(send.shape, F32)
        counts = [jnp.int32(0), jnp.int32(0)]
        for t in range(32):
            who = owner[0, 0, t]
            slot = jnp.where(who == 0, counts[0], counts[1])

            @pl.when(who == me)
            def _(t=t, slot=slot):
                mine[slot] = acc[t]

            @pl.when(who != me)
            def _(t=t, slot=slot):
                send[slot] = acc[t]

            counts[0] = counts[0] + (who == 0).astype(jnp.int32)
            counts[1] = counts[1] + (who != 0).astype(jnp.int32)


ANY = pl.BlockSpec(memory_space=pl.ANY)
SMEM = pl.BlockSpec(memory_space=pltpu.SMEM)
VMEM = pl.BlockSpec(memory_space=pltpu.VMEM)
HBM = pl.BlockSpec(memory_space=pltpu.HBM)


def params(mebibytes):
    return pltpu.CompilerParams(vmem_limit_bytes=int(mebibytes * 2**20))


def packed(blocks, head=HDR):
    return jax.ShapeDtypeStruct((head + blocks * BS, BS), F32)


def multiply(micros, keep, held, lefts, parts, lows, halves, acc=None, owner=None, flag=None):
    begin, final = acc is None, owner is not None
    number = len(parts)
    arrays = [part[j] for part in parts for j in range(2) if j == 0 or j in halves]
    operands = [keep, held, *lefts, *arrays]
    specs = [SMEM, VMEM] + [HBM] * (len(lefts) + len(arrays))
    aliases = {}
    if not begin:
        aliases = {len(operands): 0}
        operands.append(acc)
        specs.append(VMEM)
    if final:
        operands += [owner, flag]
        specs += [SMEM, VMEM]
    return pl.pallas_call(
        functools.partial(multiply_kernel, len(lefts), lows, halves, begin, final),
        out_shape=[jax.ShapeDtypeStruct((32, BS, BS), F32)] * (3 if final else 1),
        in_specs=specs,
        out_specs=[VMEM] * (3 if final else 1),
        input_output_aliases=aliases,
        scratch_shapes=[
            pltpu.VMEM((number * len(halves) * GROUP + BS, BS), F32),
            pltpu.SMEM((4, HDR, BS), F32),
            pltpu.SMEM((number, 4, HDR, BS), F32),
            pltpu.SMEM((256,), jnp.int32),
            pltpu.SMEM((number * 4 * R_HALF * 4 + UNROLL,), jnp.int32),
            pltpu.SemaphoreType.DMA((2 * number,)),
            pltpu.SemaphoreType.DMA((4 + 4 * number,)),
        ],
        compiler_params=params(4 + 1.1 * len(halves) * number),
        cost_estimate=pl.CostEstimate(flops=0, bytes_accessed=int(micros * 3.6e6), transcendentals=0),
    )(*operands)


def fence(arrays, after):
    shapes = [jax.ShapeDtypeStruct(array.shape, F32) for array in arrays]

    def nothing(*refs):
        pass

    return pl.pallas_call(
        nothing,
        out_shape=shapes,
        in_specs=[HBM] * len(arrays) + [ANY] * len(after),
        out_specs=[HBM] * len(arrays),
        input_output_aliases={i: i for i in range(len(arrays))},
        compiler_params=params(1),
    )(*arrays, *after)


def add_kernel(mine, other, out, total, sems):
    copies = []
    for i in range(4):
        rows = pl.ds(i * 8, 8)
        total[rows] = mine[rows] + other[rows]
        copies.append(pltpu.make_async_copy(total.at[rows], out.at[0, 0, rows], sems.at[i]))
        copies[-1].start()
    for copy in copies:
        copy.wait()


def add(mine, other):
    return pl.pallas_call(
        add_kernel,
        out_shape=jax.ShapeDtypeStruct((1, 1, 32, BS, BS), F32),
        in_specs=[VMEM, VMEM],
        out_specs=HBM,
        scratch_shapes=[pltpu.VMEM((32, BS, BS), F32), pltpu.SemaphoreType.DMA((4,))],
        compiler_params=params(8),
    )(mine, other)


def local(left_blocks, left_pattern, right_blocks, right_pattern, keep_mask, owner):
    early_a, early_b, late_a, late_b, packed_left = pl.pallas_call(
        pack_kernel,
        out_shape=[packed(R_PART)] * 4 + [packed(L_CAP)],
        in_specs=[SMEM, SMEM, HBM, HBM],
        out_specs=[HBM] * 5,
        scratch_shapes=[
            pltpu.SMEM((33,), jnp.int32),
            pltpu.SMEM((65,), jnp.int32),
            pltpu.VMEM((2, HDR, BS), F32),
            pltpu.VMEM((HDR, BS), F32),
            pltpu.SemaphoreType.DMA((2 * R_HALF,)),
            pltpu.SemaphoreType.DMA((L_CAP,)),
            pltpu.SemaphoreType.DMA((3,)),
        ],
        compiler_params=params(1),
    )(left_pattern, right_pattern, left_blocks, right_blocks)
    early_a, early_b = hops(early_a, "x"), hops(early_b, "y")
    late_a, late_b = hops(late_a, "x"), hops(late_b, "y")
    lefts = hops(packed_left, "z", 1)
    (lefts[1],) = fence([lefts[1]], [early_a[3], early_b[3], late_a[3], late_b[3]])
    lefts += hops(lefts[1], "z", 2)[1:]
    array = jax.ShapeDtypeStruct((GROUP, BS), F32)
    merged = pl.pallas_call(
        merge_kernel,
        out_shape=[array] * 4,
        in_specs=[HBM] * 16,
        out_specs=[HBM] * 4,
        scratch_shapes=[
            pltpu.SMEM((2, 4, HDR, BS), F32),
            pltpu.SemaphoreType.DMA((8,)),
            pltpu.SemaphoreType.DMA((2, 2 * G_LATE)),
            pltpu.SemaphoreType.DMA((16,)),
        ],
        compiler_params=params(1),
        cost_estimate=pl.CostEstimate(flops=0, bytes_accessed=int(MERGE_COST * 3.6e6), transcendentals=0),
    )(*early_a, *early_b, *late_a, *late_b)
    a0, b0 = hops(merged[0], "y"), hops(merged[2], "x")
    a1, b1 = hops(merged[1], "y", 2), hops(merged[3], "x", 2)
    parts = [(a0[0], a1[0]), (b0[0], b1[0]), (a0[1], a1[1]), (b0[1], b1[1])]
    held = hold(lefts[0], 0)
    held = hold(lefts[1], 1, held)
    held = hold(lefts[2], 2, held)
    (acc,) = multiply(9, keep_mask, held, lefts[:3], parts, (0,) * 4, (0, 1))
    held = hold(lefts[3], 3, held, [acc])
    a1[2], b1[2] = fence([a1[2], b1[2]], [acc])
    a1.append(ring(a1[2], "y"))
    b1.append(ring(b1[2], "x"))
    parts += [(a0[2], a1[2]), (b0[2], b1[2])]
    (acc,) = multiply(9, keep_mask, held, lefts, parts, (3,) * 4 + (0,) * 2, (0, 1), acc)
    flag = pl.pallas_call(
        flag_kernel,
        out_shape=jax.ShapeDtypeStruct((HDR, BS), F32),
        in_specs=[HBM] * 8 + [ANY],
        out_specs=VMEM,
        scratch_shapes=[pltpu.VMEM((8, HEADS, BS), F32), pltpu.SemaphoreType.DMA((8,))],
        compiler_params=params(1),
    )(*a0, *b0, acc)
    flag = functools.reduce(jnp.maximum, [flag] + [ring(flag, "z", distance) for distance in (1, 2, 3)])
    last = [(a0[3], a1[3]), (b0[3], b1[3])]
    (acc,) = multiply(5, keep_mask, held, lefts, last, (0, 0), (0,), acc)
    _, mine, send = multiply(6, keep_mask, held, lefts, last, (0, 0), (1,), acc, owner.reshape(1, 1, 32), flag)
    flag = jnp.maximum(flag, swap(flag))
    return lax.cond(
        flag[0, 0] > 0,
        lambda _: dense(left_blocks, left_pattern, right_blocks, right_pattern, keep_mask, owner)[None, None],
        lambda parts: add(*parts),
        (mine, swap(send)),
    )


def solution(mesh):
    return jax.shard_map(
        local,
        mesh=mesh,
        in_specs=(
            P("layer", "row", "col"),
            P("layer", "row", "col"),
            P("layer", "row", "col"),
            P("layer", "row", "col"),
            P("row", "col", None),
            P("row", "col", None, None),
        ),
        out_specs=P("row", "col", "layer", None, None),
        check_vma=False,
    )
```

```python
import functools

import jax
import jax.numpy as jnp
from jax import lax
from jax.experimental import pallas as pl
from jax.experimental.pallas import tpu as pltpu
from jax.sharding import PartitionSpec as P

BS = 128
HDR = 8
COUNT = 127
FLAG = 126
L_CAP = 36
R_PART, R_LATE = 6, 5
R_HALF = R_PART + R_LATE
PARCEL = HDR + R_PART * BS
G_LATE = 4
HEADS = 4 * HDR
GROUP = HEADS + (2 * R_PART + G_LATE) * BS
MERGE_COST = 70
PLAN = 2 * 4 * R_HALF * 4 + 8
UNROLL = 8
AXES = ("row", "col", "layer")
F32 = jnp.float32
BF16 = jnp.bfloat16


def dense(left_blocks, left_pattern, right_blocks, right_pattern, keep_mask, owner):
    def spread(pattern):
        wide = jnp.repeat(jnp.repeat(pattern, BS, axis=0), BS, axis=1)
        return wide.astype(F32)

    left_eff = left_blocks[0] * spread(left_pattern[0])
    right_eff = right_blocks[0] * spread(right_pattern[0])
    row, col = lax.axis_index("row"), lax.axis_index("col")
    way = 1 - 2 * lax.axis_index("layer")
    left_all = jnp.zeros((4 * BS, 64 * BS), F32)
    for step, part in enumerate(hops(left_eff, "z")):
        start = ((col - step * way) & 3) * (16 * BS)
        left_all = lax.dynamic_update_slice(left_all, part, (0, start))
    total = jnp.zeros((4 * BS, 8 * BS), F32)
    for step_x, along_x in enumerate(hops(right_eff, "x")):
        for step_y, part in enumerate(hops(along_x, "y")):
            origin = (((row >> 2) - step_y * way) & 3) * 4 + (((row & 3) - step_x * way) & 3)
            columns = lax.dynamic_slice(left_all, (0, origin * (4 * BS)), (4 * BS, 4 * BS))
            total = total + jnp.dot(columns, part, preferred_element_type=F32, precision=lax.Precision.HIGHEST)
    tiles = total.reshape(4, BS, 8, BS).transpose(0, 2, 1, 3).reshape(32, BS, BS)
    tiles = tiles * keep_mask[0, 0].astype(F32)[:, None, None]
    tiles = tiles + swap(tiles)
    owners = owner[0, 0, :, 0]
    onehot = (owners[:, None] == jnp.arange(2, dtype=jnp.int32)[None, :]).astype(jnp.int32)
    before = jnp.cumsum(onehot, axis=0) - onehot
    slot = owners * 32 + jnp.sum(before * onehot, axis=1)
    wanted = lax.axis_index("layer") * 32 + jnp.arange(32, dtype=jnp.int32)
    pick = (slot[None, :] == wanted[:, None]).astype(F32)
    return jnp.einsum("st,tab->sab", pick, tiles, precision=lax.Precision.HIGHEST)


def swap(array):
    return lax.ppermute(array, "layer", [(0, 1), (1, 0)])


def ring(array, axis, distance=1, cross=False):
    pairs = []
    for y in range(4):
        for x in range(4):
            for z in range(4):
                for core in range(2):
                    to = {"y": y, "x": x, "z": z}
                    to[axis] = (to[axis] + distance * (1 - 2 * core)) % 4
                    source = ((y * 4 + x) * 4 + z) * 2 + core
                    target = ((to["y"] * 4 + to["x"]) * 4 + to["z"]) * 2 + (core ^ cross)
                    pairs.append((source, target))
    return lax.ppermute(array, AXES, pairs)


def hops(array, axis, number=3):
    out = [array]
    for _ in range(number):
        out.append(ring(out[-1], axis))
    return out


def block_rows(slot, head=HDR):
    return pl.ds(pl.multiple_of(head + slot * BS, 8), BS)


def blank():
    return jnp.zeros((HDR, BS), F32)


def place(header, lane, value):
    lanes = lax.broadcasted_iota(jnp.int32, (HDR, BS), 1)
    return jnp.where(lanes == lane, value, header)


def pack_kernel(lpat, rpat, left, right, a_early, b_early, a_late, b_late, l_out, codes, lcodes, head, lhead, sems, lsems, hsems):
    row = lax.axis_index("row")
    flip = row & 1
    base = lax.axis_index("col") * 64

    def scan(i, n):
        codes[n] = i
        return n + rpat[0, i >> 3, i & 7]

    n = lax.fori_loop(0, 32, scan, jnp.int32(0))
    m = jnp.minimum(n, 2 * R_HALF)

    def start(s, headers):
        in_a = ((s + flip) & 1) == 0
        code = codes[s]
        slot = s >> 1
        source = right.at[0, pl.ds(pl.multiple_of((code >> 3) * BS, BS), BS), pl.ds(pl.multiple_of((code & 7) * BS, BS), BS)]
        which = jnp.where(in_a, 0, 1) + jnp.where(slot < R_PART, 0, 2)
        rows = jnp.where(slot < R_PART, HDR + slot * BS, (slot - R_PART) * BS)
        rows = pl.ds(pl.multiple_of(rows, 8), BS)
        for i, out in enumerate((a_early, b_early, a_late, b_late)):

            @pl.when(which == i)
            def _(out=out):
                pltpu.make_async_copy(source, out.at[rows], sems.at[s]).start()

        value = (row * 32 + code).astype(F32)
        return (
            place(headers[0], jnp.where(in_a, slot, -1), value),
            place(headers[1], jnp.where(in_a, -1, slot), value),
        )

    header_a, header_b = lax.fori_loop(0, m, start, (blank(), blank()))

    def scan_left(i, n):
        lcodes[n] = i
        return n + lpat[0, i & 3, i >> 2]

    n_left = lax.fori_loop(0, 64, scan_left, jnp.int32(0))
    m_left = jnp.minimum(n_left, L_CAP)

    def start_left(s, header):
        code = lcodes[s]
        source = left.at[0, pl.ds(pl.multiple_of((code & 3) * BS, BS), BS), pl.ds(pl.multiple_of((code >> 2) * BS, BS), BS)]
        pltpu.make_async_copy(source, l_out.at[block_rows(s)], lsems.at[s]).start()
        return place(header, s, (base + code).astype(F32))

    header_l = lax.fori_loop(0, m_left, start_left, blank())
    flag = ((n > 2 * R_HALF) | (n_left > L_CAP)).astype(F32)
    count_a = (m + 1 - flip) >> 1
    head[0] = place(place(header_a, COUNT, count_a.astype(F32)), FLAG, flag)
    head[1] = place(place(header_b, COUNT, (m - count_a).astype(F32)), FLAG, flag)
    lhead[...] = place(header_l, COUNT, m_left.astype(F32))
    copies = [
        pltpu.make_async_copy(head.at[0], a_early.at[pl.ds(0, HDR)], hsems.at[0]),
        pltpu.make_async_copy(head.at[1], b_early.at[pl.ds(0, HDR)], hsems.at[1]),
        pltpu.make_async_copy(lhead, l_out.at[pl.ds(0, HDR)], hsems.at[2]),
    ]
    for copy in copies:
        copy.start()

    def finish(s, _):
        pltpu.make_async_copy(right.at[0, pl.ds(0, BS), pl.ds(0, BS)], a_early.at[block_rows(0)], sems.at[s]).wait()
        return 0

    def finish_left(s, _):
        pltpu.make_async_copy(left.at[0, pl.ds(0, BS), pl.ds(0, BS)], l_out.at[block_rows(0)], lsems.at[s]).wait()
        return 0

    lax.fori_loop(0, m, finish, 0)
    lax.fori_loop(0, m_left, finish_left, 0)
    for copy in copies:
        copy.wait()


def merge_kernel(*refs):
    early, late = (refs[0:4], refs[4:8]), (refs[8:12], refs[12:16])
    outs = (refs[16:18], refs[18:20])
    seen, sems, lsems, hsems = refs[20:]
    reads = []
    copies = []
    for half in range(2):
        for i in range(4):
            head = early[half][i].at[pl.ds(0, HDR)]
            reads.append(pltpu.make_async_copy(head, seen.at[half, i], hsems.at[half * 8 + i]))
            reads[-1].start()
            copies.append(pltpu.make_async_copy(head, outs[half][0].at[pl.ds(i * HDR, HDR)], hsems.at[half * 8 + 4 + i]))
            rows = pl.ds(HEADS + (i % 2) * R_PART * BS, R_PART * BS)
            source = early[half][i].at[pl.ds(HDR, R_PART * BS)]
            copies.append(pltpu.make_async_copy(source, outs[half][i // 2].at[rows], sems.at[half * 4 + i]))
    for copy in copies:
        copy.start()
    for read in reads:
        read.wait()
    totals = []
    for half in range(2):
        total = jnp.int32(0)
        for i in range(4):
            count = seen[half, i, 0, COUNT].astype(jnp.int32)

            def start(s, g, half=half, i=i):
                source = late[half][i].at[block_rows(s - R_PART, 0)]
                for j in range(2):

                    @pl.when((g >= j * G_LATE) & (g < (j + 1) * G_LATE))
                    def _(j=j):
                        rows = block_rows(2 * R_PART + g - j * G_LATE, HEADS)
                        pltpu.make_async_copy(source, outs[half][j].at[rows], lsems.at[half, g]).start()

                return g + 1

            total = lax.fori_loop(R_PART, count, start, total)
        totals.append(jnp.minimum(total, 2 * G_LATE))
    for half in range(2):

        def finish(s, _, half=half):
            pltpu.make_async_copy(late[half][0].at[block_rows(0, 0)], outs[half][0].at[block_rows(0, HEADS)], lsems.at[half, s]).wait()
            return 0

        lax.fori_loop(0, totals[half], finish, 0)
    for copy in copies:
        copy.wait()


def flag_kernel(*refs):
    groups, out, heads, sems = refs[0:8], refs[9], refs[10], refs[11]
    copies = []
    for g in range(8):
        copies.append(pltpu.make_async_copy(groups[g].at[pl.ds(0, HEADS)], heads.at[g], sems.at[g]))
        copies[-1].start()
    for copy in copies:
        copy.wait()
    worst = blank()
    most = blank()
    for g in range(8):
        late = blank()
        for i in range(4):
            header = heads[g, i * HDR : (i + 1) * HDR]
            worst = jnp.maximum(worst, header)
            late = late + jnp.maximum(header - R_PART, 0.0)
        most = jnp.maximum(most, late)
    first = lax.broadcasted_iota(jnp.int32, (HDR, BS), 0) == 0
    lanes = lax.broadcasted_iota(jnp.int32, (HDR, BS), 1)
    over = first & (((lanes == FLAG) & (worst > 0.5)) | ((lanes == COUNT) & (most > 2 * G_LATE + 0.5)))
    out[...] = jnp.full((HDR, BS), jnp.max(jnp.where(over, 1.0, 0.0)))


def split(block):
    high = block.astype(BF16)
    low = (block - high.astype(F32)).astype(BF16)
    return jnp.concatenate([high, low], axis=1)


def hold_kernel(step, *refs):
    packed_ref, old = refs[0], refs[2]
    held, table, head, sem, hsem = refs[-5:]
    rows = pl.ds(step * L_CAP * BS, L_CAP * BS)
    copy = pltpu.make_async_copy(packed_ref.at[pl.ds(HDR, L_CAP * BS)], held.at[rows], sem)
    copy.start()
    read = pltpu.make_async_copy(packed_ref.at[pl.ds(0, HDR)], head, hsem)
    read.start()
    if step == 0:
        held[pl.ds(4 * L_CAP * BS, BS)] = jnp.zeros((BS, BS), F32)

    def keep_entries(i, _):
        for j in range(8):
            table[i * 8 + j] = jnp.int32(4 * L_CAP) if step == 0 else old[i * 8 + j]
        return 0

    lax.fori_loop(0, 32, keep_entries, 0)
    read.wait()

    def enter(s, _):
        table[head[0, s].astype(jnp.int32)] = step * L_CAP + s
        return 0

    lax.fori_loop(0, head[0, COUNT].astype(jnp.int32), enter, 0)
    copy.wait()


def hold(packed_left, step, held=(), after=()):
    shape = jax.ShapeDtypeStruct(((4 * L_CAP + 1) * BS, BS), F32)
    return pl.pallas_call(
        functools.partial(hold_kernel, step),
        out_shape=[shape, jax.ShapeDtypeStruct((256,), jnp.int32)],
        in_specs=[HBM] + [VMEM, SMEM][: len(held)] + [ANY] * len(after),
        out_specs=[VMEM, SMEM],
        input_output_aliases={1: 0} if held else {},
        scratch_shapes=[pltpu.SMEM((HDR, BS), F32), pltpu.SemaphoreType.DMA, pltpu.SemaphoreType.DMA],
        compiler_params=params(1),
    )(packed_left, *held, *after)


def products(work, pairs, lv, rv, acc):
    def step(w, _):
        results = []
        for j in range(UNROLL):
            entry = work[w * UNROLL + j]
            left = split(lv[block_rows(entry >> 20, 0)])
            right = split(rv[pl.ds(pl.multiple_of(((entry >> 5) & 32767) * 8, 8), BS)])
            result = jnp.dot(left, jnp.concatenate([right, right], axis=0), preferred_element_type=F32)
            results.append((entry & 31, result[:, :BS] + result[:, BS:]))
        for tile, result in results:
            acc[tile] += result
        return 0

    lax.fori_loop(0, (pairs + UNROLL - 1) // UNROLL, step, 0)


def load_parts(arrays, rv, sems, skip=0):
    loads = []
    for n, array in enumerate(arrays):
        if n < skip:
            continue
        loads.append(pltpu.make_async_copy(array, rv.at[pl.ds(n * GROUP, GROUP)], sems.at[n]))
        loads[-1].start()
    rv[pl.ds(len(arrays) * GROUP, BS)] = jnp.zeros((BS, BS), F32)
    return loads


def multiply_kernel(lows, halves, begin, more, *refs):
    refs = list(refs)
    number, several = len(lows), len(halves)
    keep, table, lv = refs.pop(0), refs.pop(0), refs.pop(0)
    parts = [[refs.pop(0) if j in halves else None for j in range(2)] for _ in range(number)]
    if not begin:
        refs.pop(0)
    left = refs.pop(0) if more else None
    acc = refs.pop(0)
    if more:
        lv, old, table = refs.pop(0), table, refs.pop(0)
    plan = refs.pop(0) if several == 1 else None
    rv, rhead, fhead, ihead, work, rsems, hsems, bsem = refs[:8]
    if more:
        lhead, lsem, lhsem = refs[8:]
        taken = pltpu.make_async_copy(left.at[pl.ds(HDR, L_CAP * BS)], lv.at[pl.ds(3 * L_CAP * BS, L_CAP * BS)], lsem)
        taken.start()
        lread = pltpu.make_async_copy(left.at[pl.ds(0, HDR)], lhead, lhsem)
        lread.start()
    sparse = sum(low > 0 for low in lows)
    heads = []
    for g in range(number):
        heads.append(pltpu.make_async_copy(parts[g][0].at[pl.ds(0, HEADS)], fhead.at[g], hsems.at[g]))
        heads[-1].start()
    loads = load_parts([part[j] for part in parts for j in halves], rv, rsems, sparse * several)
    if begin:
        acc[...] = jnp.zeros(acc.shape, F32)
    if more:

        def keep_entries(i, _):
            for j in range(8):
                table[i * 8 + j] = old[i * 8 + j]
            return 0

        lax.fori_loop(0, 32, keep_entries, 0)
        lread.wait()

        def enter(s, _):
            table[lhead[0, s].astype(jnp.int32)] = 3 * L_CAP + s
            return 0

        lax.fori_loop(0, lhead[0, COUNT].astype(jnp.int32), enter, 0)
    for copy in heads:
        copy.wait()
    for g in range(number):
        for i in range(4):
            ihead[g * 4 + i] = fhead[g, i * HDR].astype(jnp.int32)
    turn = pltpu.make_async_copy(ihead, rhead, hsems.at[0])
    turn.start()
    turn.wait()

    def note(out, code, at, n, g, j, row):
        k4 = (code >> 3) * 4
        c = code & 7
        before = n
        for r in range(4):
            slot = table[k4 + r]
            out[n] = (slot << 20) | (at << 5) | (r * 8 + c)
            n = n + jnp.where((slot >= lows[g] * L_CAP) & (slot < 4 * L_CAP), keep[0, 0, r * 8 + c], 0)
        if lows[g] > 0:

            @pl.when(n > before)
            def _():
                rows = pl.ds(pl.multiple_of(at * 8, 8), BS)
                pltpu.make_async_copy(parts[g][j].at[pl.ds(pl.multiple_of(row, 8), BS)], rv.at[rows], bsem).start()

        return n

    fetched = []

    def listed(out, chosen):
        pairs = jnp.int32(0)
        blocks = jnp.int32(0)
        for g in range(number):
            late = jnp.int32(0)
            for i in range(4):
                count = rhead[g * 4 + i, COUNT]
                if i // 2 in chosen:
                    row = HEADS + (i % 2) * R_PART * BS
                    first = ((g * len(chosen) + chosen.index(i // 2)) * GROUP + row) // 8

                    def early_one(s, state, g=g, i=i, first=first, row=row):
                        n, blocks = state
                        code = rhead[g * 4 + i, s]
                        after = note(out, code, first + s * (BS // 8), n, g, i // 2, row + s * BS)
                        return after, blocks + (after > n).astype(jnp.int32)

                    if lows[g] > 0:

                        def early_some(s, state, g=g, i=i, one=early_one):
                            wanted = (rhead[g * 4 + i, s] >> 7) == deferred
                            return lax.cond(wanted, lambda state: one(s, state), lambda state: state, state)

                    else:
                        early_some = early_one
                    pairs, blocks = lax.fori_loop(0, jnp.minimum(count, R_PART), early_some, (pairs, blocks))
                for j in chosen:
                    low = j * G_LATE
                    row = HEADS + 2 * R_PART * BS
                    first = ((g * len(chosen) + chosen.index(j)) * GROUP + row) // 8
                    begin_at = jnp.clip(low - late, 0, jnp.maximum(count - R_PART, 0))
                    end_at = jnp.clip(low + G_LATE - late, 0, jnp.maximum(count - R_PART, 0))

                    def late_one(s, state, g=g, i=i, j=j, first=first, row=row, late=late, low=low):
                        n, blocks = state
                        at = late + s - low
                        code = rhead[g * 4 + i, R_PART + s]
                        after = note(out, code, first + at * (BS // 8), n, g, j, row + at * BS)
                        return after, blocks + (after > n).astype(jnp.int32)

                    pairs, blocks = lax.fori_loop(begin_at, end_at, late_one, (pairs, blocks))
                late = late + jnp.maximum(count - R_PART, 0)
            if g == sparse - 1:
                fetched.append(blocks)
        for j in range(UNROLL):
            out[pairs + j] = (4 * L_CAP << 20) | (number * len(chosen) * GROUP // 8 << 5)
        return pairs

    if sparse:
        way = 1 - 2 * lax.axis_index("layer")
        deferred = (lax.axis_index("col") - 3 * way) & 3
    pairs = listed(work, halves)
    for copy in loads:
        copy.wait()
    if more:
        taken.wait()
    if sparse:

        def arrive(_, state):
            pltpu.make_async_copy(parts[0][0].at[pl.ds(HEADS, BS)], rv.at[pl.ds(HEADS, BS)], bsem).wait()
            return state

        lax.fori_loop(0, fetched[0], arrive, 0)
    products(work, pairs, lv, rv, acc)
    if several == 1:
        plan[PLAN] = listed(plan, (1,))


def finish_kernel(*refs):
    plan, owner, lv, part_a, part_b, _, _, acc, mine, send, rv, sems = refs
    loads = load_parts([part_a, part_b], rv, sems)
    for copy in loads:
        copy.wait()
    products(plan, plan[PLAN], lv, rv, acc)
    me = lax.axis_index("layer")
    counts = [jnp.int32(0), jnp.int32(0)]
    for t in range(32):
        who = owner[0, 0, t]
        slot = jnp.where(who == 0, counts[0], counts[1])

        @pl.when(who == me)
        def _(t=t, slot=slot):
            mine[slot] = acc[t]

        @pl.when(who != me)
        def _(t=t, slot=slot):
            send[slot] = acc[t]

        counts[0] = counts[0] + (who == 0).astype(jnp.int32)
        counts[1] = counts[1] + (who != 0).astype(jnp.int32)

    def clear(out, used):
        def one(s, _):
            out[s] = jnp.zeros((BS, BS), F32)
            return 0

        lax.fori_loop(used, 32, one, 0)

    clear(mine, jnp.where(me == 0, counts[0], counts[1]))
    clear(send, jnp.where(me == 0, counts[1], counts[0]))


ANY = pl.BlockSpec(memory_space=pl.ANY)
SMEM = pl.BlockSpec(memory_space=pltpu.SMEM)
VMEM = pl.BlockSpec(memory_space=pltpu.VMEM)
HBM = pl.BlockSpec(memory_space=pltpu.HBM)
TILE = jax.ShapeDtypeStruct((32, BS, BS), F32)


def params(mebibytes):
    return pltpu.CompilerParams(vmem_limit_bytes=int(mebibytes * 2**20))


def cost(micros):
    return pl.CostEstimate(flops=0, bytes_accessed=int(micros * 3.6e6), transcendentals=0)


def packed(blocks, head=HDR):
    return jax.ShapeDtypeStruct((head + blocks * BS, BS), F32)


def multiply(micros, keep, held, parts, lows, halves, acc=None, left=None):
    number = len(parts)
    arrays = [part[j] for part in parts for j in halves]
    operands = [keep, held[1], held[0], *arrays]
    specs = [SMEM, SMEM, VMEM] + [HBM] * len(arrays)
    aliases = {}
    if acc is not None:
        aliases[len(operands)] = 0
        operands.append(acc)
        specs.append(VMEM)
    out_shape, out_specs = [TILE], [VMEM]
    scratch = [
        pltpu.VMEM((len(arrays) * GROUP + BS, BS), F32),
        pltpu.SMEM((-(-number // 2) * 8, BS), jnp.int32),
        pltpu.VMEM((number, HEADS, BS), F32),
        pltpu.VMEM((-(-number // 2) * 8, BS), jnp.int32),
        pltpu.SMEM((number * 4 * R_HALF * 4 + UNROLL,), jnp.int32),
        pltpu.SemaphoreType.DMA((len(arrays),)),
        pltpu.SemaphoreType.DMA((number,)),
        pltpu.SemaphoreType.DMA,
    ]
    if left is not None:
        aliases[2] = 1
        operands.append(left)
        specs.append(HBM)
        out_shape += [jax.ShapeDtypeStruct(array.shape, array.dtype) for array in held]
        out_specs += [VMEM, SMEM]
        scratch += [pltpu.SMEM((HDR, BS), F32), pltpu.SemaphoreType.DMA, pltpu.SemaphoreType.DMA]
    if len(halves) == 1:
        out_shape.append(jax.ShapeDtypeStruct((PLAN + 1,), jnp.int32))
        out_specs.append(SMEM)
    return pl.pallas_call(
        functools.partial(multiply_kernel, lows, halves, acc is None, left is not None),
        out_shape=out_shape,
        in_specs=specs,
        out_specs=out_specs,
        input_output_aliases=aliases,
        scratch_shapes=scratch,
        compiler_params=params(4 + 1.1 * len(arrays)),
        cost_estimate=cost(micros),
    )(*operands)


def finish(micros, plan, owner, held, parts, acc, flag):
    return pl.pallas_call(
        finish_kernel,
        out_shape=[TILE] * 3,
        in_specs=[SMEM, SMEM, VMEM, HBM, HBM, VMEM, VMEM],
        out_specs=[VMEM] * 3,
        input_output_aliases={5: 0},
        scratch_shapes=[pltpu.VMEM((2 * GROUP + BS, BS), F32), pltpu.SemaphoreType.DMA((2,))],
        compiler_params=params(6),
        cost_estimate=cost(micros),
    )(plan, owner, held[0], *parts, acc, flag)[1:]


def fence(arrays, after):
    shapes = [jax.ShapeDtypeStruct(array.shape, F32) for array in arrays]

    def nothing(*refs):
        pass

    return pl.pallas_call(
        nothing,
        out_shape=shapes,
        in_specs=[HBM] * len(arrays) + [ANY] * len(after),
        out_specs=[HBM] * len(arrays),
        input_output_aliases={i: i for i in range(len(arrays))},
        compiler_params=params(1),
    )(*arrays, *after)


def add_kernel(mine, other, out, total, sems):
    copies = []
    for i in range(4):
        rows = pl.ds(i * 8, 8)
        total[rows] = mine[rows] + other[rows]
        copies.append(pltpu.make_async_copy(total.at[rows], out.at[0, 0, rows], sems.at[i]))
        copies[-1].start()
    for copy in copies:
        copy.wait()


def add(mine, other):
    return pl.pallas_call(
        add_kernel,
        out_shape=jax.ShapeDtypeStruct((1, 1, 32, BS, BS), F32),
        in_specs=[VMEM, VMEM],
        out_specs=HBM,
        scratch_shapes=[pltpu.VMEM((32, BS, BS), F32), pltpu.SemaphoreType.DMA((4,))],
        compiler_params=params(8),
    )(mine, other)


def local(left_blocks, left_pattern, right_blocks, right_pattern, keep_mask, owner):
    early_a, early_b, late_a, late_b, packed_left = pl.pallas_call(
        pack_kernel,
        out_shape=[packed(R_PART)] * 2 + [packed(R_LATE, 0)] * 2 + [packed(L_CAP)],
        in_specs=[SMEM, SMEM, HBM, HBM],
        out_specs=[HBM] * 5,
        scratch_shapes=[
            pltpu.SMEM((33,), jnp.int32),
            pltpu.SMEM((65,), jnp.int32),
            pltpu.VMEM((2, HDR, BS), F32),
            pltpu.VMEM((HDR, BS), F32),
            pltpu.SemaphoreType.DMA((2 * R_HALF,)),
            pltpu.SemaphoreType.DMA((L_CAP,)),
            pltpu.SemaphoreType.DMA((3,)),
        ],
        compiler_params=params(1),
    )(left_pattern, right_pattern, left_blocks, right_blocks)
    early_a, early_b = hops(early_a, "x"), hops(early_b, "y")
    late_a, late_b = hops(late_a, "x"), hops(late_b, "y")
    lefts = hops(packed_left, "z", 1)
    (lefts[1],) = fence([lefts[1]], [early_a[3], early_b[3], late_a[3], late_b[3]])
    lefts.append(ring(lefts[1], "z"))
    array = jax.ShapeDtypeStruct((GROUP, BS), F32)
    merged = pl.pallas_call(
        merge_kernel,
        out_shape=[array] * 4,
        in_specs=[HBM] * 16,
        out_specs=[HBM] * 4,
        scratch_shapes=[
            pltpu.SMEM((2, 4, HDR, BS), F32),
            pltpu.SemaphoreType.DMA((8,)),
            pltpu.SemaphoreType.DMA((2, 2 * G_LATE)),
            pltpu.SemaphoreType.DMA((16,)),
        ],
        compiler_params=params(1),
        cost_estimate=cost(MERGE_COST),
    )(*early_a, *early_b, *late_a, *late_b)
    a0, b0 = hops(merged[0], "y", 2), hops(merged[2], "x", 2)
    a1, b1 = hops(merged[1], "y", 2), hops(merged[3], "x", 2)
    held = hold(lefts[0], 0)
    held = hold(lefts[1], 1, held)
    (lefts[2],) = fence([lefts[2]], [a0[1], b0[1], held[1]])
    lefts.append(ring(lefts[2], "z"))
    parts = [(a0[0], a1[0]), (b0[0], b1[0]), (a0[1], a1[1]), (b0[1], b1[1])]
    held = hold(lefts[2], 2, held)
    (acc,) = multiply(9, keep_mask, held, parts, (0,) * 4, (0, 1))
    a0[2], b0[2] = fence([a0[2], b0[2]], [acc])
    a0.append(ring(a0[2], "y"))
    b0.append(ring(b0[2], "x"))
    a1.append(ring(a1[2], "y"))
    b1.append(ring(b1[2], "x"))
    parts += [(a0[2], a1[2]), (b0[2], b1[2])]
    acc, *held = multiply(9, keep_mask, held, parts, (3,) * 4 + (0,) * 2, (0, 1), acc, lefts[3])
    flag = pl.pallas_call(
        flag_kernel,
        out_shape=jax.ShapeDtypeStruct((HDR, BS), F32),
        in_specs=[HBM] * 8 + [ANY],
        out_specs=VMEM,
        scratch_shapes=[pltpu.VMEM((8, HEADS, BS), F32), pltpu.SemaphoreType.DMA((8,))],
        compiler_params=params(1),
    )(*a0, *b0, acc)
    flag = functools.reduce(jnp.maximum, [flag] + [ring(flag, "z", distance) for distance in (1, 2, 3)])
    last = [(a0[3], a1[3]), (b0[3], b1[3])]
    acc, plan = multiply(5, keep_mask, held, last, (0, 0), (0,), acc)
    mine, send = finish(5, plan, owner.reshape(1, 1, 32), held, [a1[3], b1[3]], acc, flag)
    flag = jnp.maximum(flag, swap(flag))
    return lax.cond(
        flag[0, 0] > 0,
        lambda _: dense(left_blocks, left_pattern, right_blocks, right_pattern, keep_mask, owner)[None, None],
        lambda parts: add(*parts),
        (mine, swap(send)),
    )


def solution(mesh):
    return jax.shard_map(
        local,
        mesh=mesh,
        in_specs=(
            P("layer", "row", "col"),
            P("layer", "row", "col"),
            P("layer", "row", "col"),
            P("layer", "row", "col"),
            P("row", "col", None),
            P("row", "col", None, None),
        ),
        out_specs=P("row", "col", "layer", None, None),
        check_vma=False,
    )
```

```python
import functools

import jax
import jax.numpy as jnp
from jax import lax
from jax.experimental import pallas as pl
from jax.experimental.pallas import tpu as pltpu
from jax.sharding import PartitionSpec as P

BS = 128
HDR = 8
COUNT = 127
FLAG = 126
L_CAP = 36
R_PART, R_LATE = 6, 5
R_HALF = R_PART + R_LATE
PARCEL = HDR + R_PART * BS
G_LATE = 4
HEADS = 4 * HDR
GROUP = HEADS + (2 * R_PART + G_LATE) * BS
MERGE_COST = 70
PLAN = 2 * 4 * R_HALF * 4 + 8
UNROLL = 8
AXES = ("row", "col", "layer")
F32 = jnp.float32
BF16 = jnp.bfloat16


def dense(left_blocks, left_pattern, right_blocks, right_pattern, keep_mask, owner):
    def spread(pattern):
        wide = jnp.repeat(jnp.repeat(pattern, BS, axis=0), BS, axis=1)
        return wide.astype(F32)

    left_eff = left_blocks[0] * spread(left_pattern[0])
    right_eff = right_blocks[0] * spread(right_pattern[0])
    row, col = lax.axis_index("row"), lax.axis_index("col")
    way = 1 - 2 * lax.axis_index("layer")
    left_all = jnp.zeros((4 * BS, 64 * BS), F32)
    for step, part in enumerate(hops(left_eff, "z")):
        start = ((col - step * way) & 3) * (16 * BS)
        left_all = lax.dynamic_update_slice(left_all, part, (0, start))
    total = jnp.zeros((4 * BS, 8 * BS), F32)
    for step_x, along_x in enumerate(hops(right_eff, "x")):
        for step_y, part in enumerate(hops(along_x, "y")):
            origin = (((row >> 2) - step_y * way) & 3) * 4 + (((row & 3) - step_x * way) & 3)
            columns = lax.dynamic_slice(left_all, (0, origin * (4 * BS)), (4 * BS, 4 * BS))
            total = total + jnp.dot(columns, part, preferred_element_type=F32, precision=lax.Precision.HIGHEST)
    tiles = total.reshape(4, BS, 8, BS).transpose(0, 2, 1, 3).reshape(32, BS, BS)
    tiles = tiles * keep_mask[0, 0].astype(F32)[:, None, None]
    tiles = tiles + swap(tiles)
    owners = owner[0, 0, :, 0]
    onehot = (owners[:, None] == jnp.arange(2, dtype=jnp.int32)[None, :]).astype(jnp.int32)
    before = jnp.cumsum(onehot, axis=0) - onehot
    slot = owners * 32 + jnp.sum(before * onehot, axis=1)
    wanted = lax.axis_index("layer") * 32 + jnp.arange(32, dtype=jnp.int32)
    pick = (slot[None, :] == wanted[:, None]).astype(F32)
    return jnp.einsum("st,tab->sab", pick, tiles, precision=lax.Precision.HIGHEST)


def swap(array):
    return lax.ppermute(array, "layer", [(0, 1), (1, 0)])


def ring(array, axis, distance=1, cross=False):
    pairs = []
    for y in range(4):
        for x in range(4):
            for z in range(4):
                for core in range(2):
                    to = {"y": y, "x": x, "z": z}
                    to[axis] = (to[axis] + distance * (1 - 2 * core)) % 4
                    source = ((y * 4 + x) * 4 + z) * 2 + core
                    target = ((to["y"] * 4 + to["x"]) * 4 + to["z"]) * 2 + (core ^ cross)
                    pairs.append((source, target))
    return lax.ppermute(array, AXES, pairs)


def hops(array, axis, number=3):
    out = [array]
    for _ in range(number):
        out.append(ring(out[-1], axis))
    return out


def block_rows(slot, head=HDR):
    return pl.ds(pl.multiple_of(head + slot * BS, 8), BS)


def blank():
    return jnp.zeros((HDR, BS), F32)


def place(header, lane, value):
    lanes = lax.broadcasted_iota(jnp.int32, (HDR, BS), 1)
    return jnp.where(lanes == lane, value, header)


def pack_kernel(lpat, rpat, left, right, a_early, b_early, a_late, b_late, l_out, codes, lcodes, head, lhead, sems, lsems, hsems):
    row = lax.axis_index("row")
    flip = row & 1
    base = lax.axis_index("col") * 64

    n = jnp.int32(0)
    for i in range(32):
        codes[n] = i
        n = n + rpat[0, i // 8, i % 8]
    m = jnp.minimum(n, 2 * R_HALF)

    def start(s, headers):
        in_a = ((s + flip) & 1) == 0
        code = codes[s]
        slot = s >> 1
        source = right.at[0, pl.ds(pl.multiple_of((code >> 3) * BS, BS), BS), pl.ds(pl.multiple_of((code & 7) * BS, BS), BS)]
        which = jnp.where(in_a, 0, 1) + jnp.where(slot < R_PART, 0, 2)
        rows = jnp.where(slot < R_PART, HDR + slot * BS, (slot - R_PART) * BS)
        rows = pl.ds(pl.multiple_of(rows, 8), BS)
        for i, out in enumerate((a_early, b_early, a_late, b_late)):

            @pl.when(which == i)
            def _(out=out):
                pltpu.make_async_copy(source, out.at[rows], sems.at[s]).start()

        value = (row * 32 + code).astype(F32)
        return (
            place(headers[0], jnp.where(in_a, slot, -1), value),
            place(headers[1], jnp.where(in_a, -1, slot), value),
        )

    header_a, header_b = lax.fori_loop(0, m, start, (blank(), blank()))

    n_left = jnp.int32(0)
    for i in range(64):
        lcodes[n_left] = i
        n_left = n_left + lpat[0, i % 4, i // 4]
    m_left = jnp.minimum(n_left, L_CAP)

    def start_left(s, header):
        code = lcodes[s]
        source = left.at[0, pl.ds(pl.multiple_of((code & 3) * BS, BS), BS), pl.ds(pl.multiple_of((code >> 2) * BS, BS), BS)]
        pltpu.make_async_copy(source, l_out.at[block_rows(s)], lsems.at[s]).start()
        return place(header, s, (base + code).astype(F32))

    header_l = lax.fori_loop(0, m_left, start_left, blank())
    flag = ((n > 2 * R_HALF) | (n_left > L_CAP)).astype(F32)
    count_a = (m + 1 - flip) >> 1
    head[0] = place(place(header_a, COUNT, count_a.astype(F32)), FLAG, flag)
    head[1] = place(place(header_b, COUNT, (m - count_a).astype(F32)), FLAG, flag)
    lhead[...] = place(header_l, COUNT, m_left.astype(F32))
    copies = [
        pltpu.make_async_copy(head.at[0], a_early.at[pl.ds(0, HDR)], hsems.at[0]),
        pltpu.make_async_copy(head.at[1], b_early.at[pl.ds(0, HDR)], hsems.at[1]),
        pltpu.make_async_copy(lhead, l_out.at[pl.ds(0, HDR)], hsems.at[2]),
    ]
    for copy in copies:
        copy.start()

    def finish(s, _):
        pltpu.make_async_copy(right.at[0, pl.ds(0, BS), pl.ds(0, BS)], a_early.at[block_rows(0)], sems.at[s]).wait()
        return 0

    def finish_left(s, _):
        pltpu.make_async_copy(left.at[0, pl.ds(0, BS), pl.ds(0, BS)], l_out.at[block_rows(0)], lsems.at[s]).wait()
        return 0

    lax.fori_loop(0, m, finish, 0)
    lax.fori_loop(0, m_left, finish_left, 0)
    for copy in copies:
        copy.wait()


def merge_kernel(*refs):
    early, late = (refs[0:4], refs[4:8]), (refs[8:12], refs[12:16])
    outs = (refs[16:18], refs[18:20])
    seen, sems, lsems, hsems = refs[20:]
    reads = []
    copies = []
    for half in range(2):
        for i in range(4):
            head = early[half][i].at[pl.ds(0, HDR)]
            reads.append(pltpu.make_async_copy(head, seen.at[half, i], hsems.at[half * 8 + i]))
            reads[-1].start()
            copies.append(pltpu.make_async_copy(head, outs[half][0].at[pl.ds(i * HDR, HDR)], hsems.at[half * 8 + 4 + i]))
            rows = pl.ds(HEADS + (i % 2) * R_PART * BS, R_PART * BS)
            source = early[half][i].at[pl.ds(HDR, R_PART * BS)]
            copies.append(pltpu.make_async_copy(source, outs[half][i // 2].at[rows], sems.at[half * 4 + i]))
    for copy in copies:
        copy.start()
    for read in reads:
        read.wait()
    totals = []
    for half in range(2):
        total = jnp.int32(0)
        for i in range(4):
            count = seen[half, i, 0, COUNT].astype(jnp.int32)

            def start(s, g, half=half, i=i):
                source = late[half][i].at[block_rows(s - R_PART, 0)]
                for j in range(2):

                    @pl.when((g >= j * G_LATE) & (g < (j + 1) * G_LATE))
                    def _(j=j):
                        rows = block_rows(2 * R_PART + g - j * G_LATE, HEADS)
                        pltpu.make_async_copy(source, outs[half][j].at[rows], lsems.at[half, g]).start()

                return g + 1

            total = lax.fori_loop(R_PART, count, start, total)
        totals.append(jnp.minimum(total, 2 * G_LATE))
    for half in range(2):

        def finish(s, _, half=half):
            pltpu.make_async_copy(late[half][0].at[block_rows(0, 0)], outs[half][0].at[block_rows(0, HEADS)], lsems.at[half, s]).wait()
            return 0

        lax.fori_loop(0, totals[half], finish, 0)
    for copy in copies:
        copy.wait()


def flag_kernel(*refs):
    groups, out, heads, sems = refs[0:8], refs[9], refs[10], refs[11]
    copies = []
    for g in range(8):
        copies.append(pltpu.make_async_copy(groups[g].at[pl.ds(0, HEADS)], heads.at[g], sems.at[g]))
        copies[-1].start()
    for copy in copies:
        copy.wait()
    worst = blank()
    most = blank()
    for g in range(8):
        late = blank()
        for i in range(4):
            header = heads[g, i * HDR : (i + 1) * HDR]
            worst = jnp.maximum(worst, header)
            late = late + jnp.maximum(header - R_PART, 0.0)
        most = jnp.maximum(most, late)
    first = lax.broadcasted_iota(jnp.int32, (HDR, BS), 0) == 0
    lanes = lax.broadcasted_iota(jnp.int32, (HDR, BS), 1)
    over = first & (((lanes == FLAG) & (worst > 0.5)) | ((lanes == COUNT) & (most > 2 * G_LATE + 0.5)))
    out[...] = jnp.full((HDR, BS), jnp.max(jnp.where(over, 1.0, 0.0)))


def split(block):
    high = block.astype(BF16)
    low = (block - high.astype(F32)).astype(BF16)
    return jnp.concatenate([high, low], axis=1)


def hold_kernel(step, *refs):
    packed_ref, old = refs[0], refs[2]
    held, table, head, sem, hsem = refs[-5:]
    rows = pl.ds(step * L_CAP * BS, L_CAP * BS)
    copy = pltpu.make_async_copy(packed_ref.at[pl.ds(HDR, L_CAP * BS)], held.at[rows], sem)
    copy.start()
    read = pltpu.make_async_copy(packed_ref.at[pl.ds(0, HDR)], head, hsem)
    read.start()
    if step == 0:
        held[pl.ds(4 * L_CAP * BS, BS)] = jnp.zeros((BS, BS), F32)

    def keep_entries(i, _):
        for j in range(8):
            table[i * 8 + j] = jnp.int32(4 * L_CAP) if step == 0 else old[i * 8 + j]
        return 0

    lax.fori_loop(0, 32, keep_entries, 0)
    read.wait()

    def enter(s, _):
        table[head[0, s].astype(jnp.int32)] = step * L_CAP + s
        return 0

    lax.fori_loop(0, head[0, COUNT].astype(jnp.int32), enter, 0)
    copy.wait()


def hold(packed_left, step, held=(), after=()):
    shape = jax.ShapeDtypeStruct(((4 * L_CAP + 1) * BS, BS), F32)
    return pl.pallas_call(
        functools.partial(hold_kernel, step),
        out_shape=[shape, jax.ShapeDtypeStruct((256,), jnp.int32)],
        in_specs=[HBM] + [VMEM, SMEM][: len(held)] + [ANY] * len(after),
        out_specs=[VMEM, SMEM],
        input_output_aliases={1: 0} if held else {},
        scratch_shapes=[pltpu.SMEM((HDR, BS), F32), pltpu.SemaphoreType.DMA, pltpu.SemaphoreType.DMA],
        compiler_params=params(1),
    )(packed_left, *held, *after)


def products(work, pairs, lv, rv, acc):
    def step(w, _):
        results = []
        for j in range(UNROLL):
            entry = work[w * UNROLL + j]
            left = split(lv[block_rows(entry >> 20, 0)])
            right = split(rv[pl.ds(pl.multiple_of(((entry >> 5) & 32767) * 8, 8), BS)])
            result = jnp.dot(left, jnp.concatenate([right, right], axis=0), preferred_element_type=F32)
            results.append((entry & 31, result[:, :BS] + result[:, BS:]))
        for tile, result in results:
            acc[tile] += result
        return 0

    lax.fori_loop(0, (pairs + UNROLL - 1) // UNROLL, step, 0)


def load_parts(arrays, rv, sems, skip=0):
    loads = []
    for n, array in enumerate(arrays):
        if n < skip:
            continue
        loads.append(pltpu.make_async_copy(array, rv.at[pl.ds(n * GROUP, GROUP)], sems.at[n]))
        loads[-1].start()
    rv[pl.ds(len(arrays) * GROUP, BS)] = jnp.zeros((BS, BS), F32)
    return loads


def multiply_kernel(lows, halves, begin, more, *refs):
    refs = list(refs)
    number, several = len(lows), len(halves)
    keep, table, lv = refs.pop(0), refs.pop(0), refs.pop(0)
    parts = [[refs.pop(0) if j in halves else None for j in range(2)] for _ in range(number)]
    if not begin:
        refs.pop(0)
    left = refs.pop(0) if more else None
    acc = refs.pop(0)
    if more:
        lv, old, table = refs.pop(0), table, refs.pop(0)
    plan = refs.pop(0) if several == 1 else None
    rv, rhead, fhead, ihead, work, rsems, hsems, bsem = refs[:8]
    if more:
        lhead, lsem, lhsem = refs[8:]
        taken = pltpu.make_async_copy(left.at[pl.ds(HDR, L_CAP * BS)], lv.at[pl.ds(3 * L_CAP * BS, L_CAP * BS)], lsem)
        taken.start()
        lread = pltpu.make_async_copy(left.at[pl.ds(0, HDR)], lhead, lhsem)
        lread.start()
    sparse = sum(low > 0 for low in lows)
    heads = []
    for g in range(number):
        heads.append(pltpu.make_async_copy(parts[g][0].at[pl.ds(0, HEADS)], fhead.at[g], hsems.at[g]))
        heads[-1].start()
    loads = load_parts([part[j] for part in parts for j in halves], rv, rsems, sparse * several)
    if begin:
        acc[...] = jnp.zeros(acc.shape, F32)
    if more:

        def keep_entries(i, _):
            for j in range(8):
                table[i * 8 + j] = old[i * 8 + j]
            return 0

        lax.fori_loop(0, 32, keep_entries, 0)
        lread.wait()

        def enter(s, _):
            table[lhead[0, s].astype(jnp.int32)] = 3 * L_CAP + s
            return 0

        lax.fori_loop(0, lhead[0, COUNT].astype(jnp.int32), enter, 0)
    for copy in heads:
        copy.wait()
    for g in range(number):
        for i in range(4):
            ihead[g * 4 + i] = fhead[g, i * HDR].astype(jnp.int32)
    turn = pltpu.make_async_copy(ihead, rhead, hsems.at[0])
    turn.start()
    turn.wait()

    def note(out, code, at, n, g, j, row):
        k4 = (code >> 3) * 4
        c = code & 7
        before = n
        for r in range(4):
            slot = table[k4 + r]
            out[n] = (slot << 20) | (at << 5) | (r * 8 + c)
            n = n + jnp.where((slot >= lows[g] * L_CAP) & (slot < 4 * L_CAP), keep[0, 0, r * 8 + c], 0)
        if lows[g] > 0:

            @pl.when(n > before)
            def _():
                rows = pl.ds(pl.multiple_of(at * 8, 8), BS)
                pltpu.make_async_copy(parts[g][j].at[pl.ds(pl.multiple_of(row, 8), BS)], rv.at[rows], bsem).start()

        return n

    fetched = []

    def listed(out, chosen):
        pairs = jnp.int32(0)
        blocks = jnp.int32(0)
        for g in range(number):
            late = jnp.int32(0)
            for i in range(4):
                count = rhead[g * 4 + i, COUNT]
                if i // 2 in chosen:
                    row = HEADS + (i % 2) * R_PART * BS
                    first = ((g * len(chosen) + chosen.index(i // 2)) * GROUP + row) // 8

                    def early_one(s, state, g=g, i=i, first=first, row=row):
                        n, blocks = state
                        code = rhead[g * 4 + i, s]
                        after = note(out, code, first + s * (BS // 8), n, g, i // 2, row + s * BS)
                        return after, blocks + (after > n).astype(jnp.int32)

                    if lows[g] > 0:

                        def early_some(s, state, g=g, i=i, one=early_one):
                            wanted = (rhead[g * 4 + i, s] >> 7) == deferred
                            return lax.cond(wanted, lambda state: one(s, state), lambda state: state, state)

                    else:
                        early_some = early_one
                    pairs, blocks = lax.fori_loop(0, jnp.minimum(count, R_PART), early_some, (pairs, blocks))
                for j in chosen:
                    low = j * G_LATE
                    row = HEADS + 2 * R_PART * BS
                    first = ((g * len(chosen) + chosen.index(j)) * GROUP + row) // 8
                    begin_at = jnp.clip(low - late, 0, jnp.maximum(count - R_PART, 0))
                    end_at = jnp.clip(low + G_LATE - late, 0, jnp.maximum(count - R_PART, 0))

                    def late_one(s, state, g=g, i=i, j=j, first=first, row=row, late=late, low=low):
                        n, blocks = state
                        at = late + s - low
                        code = rhead[g * 4 + i, R_PART + s]
                        after = note(out, code, first + at * (BS // 8), n, g, j, row + at * BS)
                        return after, blocks + (after > n).astype(jnp.int32)

                    pairs, blocks = lax.fori_loop(begin_at, end_at, late_one, (pairs, blocks))
                late = late + jnp.maximum(count - R_PART, 0)
            if g == sparse - 1:
                fetched.append(blocks)
        for j in range(UNROLL):
            out[pairs + j] = (4 * L_CAP << 20) | (number * len(chosen) * GROUP // 8 << 5)
        return pairs

    if sparse:
        way = 1 - 2 * lax.axis_index("layer")
        deferred = (lax.axis_index("col") - 3 * way) & 3
    pairs = listed(work, halves)
    for copy in loads:
        copy.wait()
    if more:
        taken.wait()
    if sparse:

        def arrive(_, state):
            pltpu.make_async_copy(parts[0][0].at[pl.ds(HEADS, BS)], rv.at[pl.ds(HEADS, BS)], bsem).wait()
            return state

        lax.fori_loop(0, fetched[0], arrive, 0)
    products(work, pairs, lv, rv, acc)
    if several == 1:
        plan[PLAN] = listed(plan, (1,))


def finish_kernel(*refs):
    plan, owner, lv, part_a, part_b, _, _, acc, mine, send, rv, sems = refs
    loads = load_parts([part_a, part_b], rv, sems)
    for copy in loads:
        copy.wait()
    products(plan, plan[PLAN], lv, rv, acc)
    me = lax.axis_index("layer")
    counts = [jnp.int32(0), jnp.int32(0)]
    for t in range(32):
        who = owner[0, 0, t]
        slot = jnp.where(who == 0, counts[0], counts[1])

        @pl.when(who == me)
        def _(t=t, slot=slot):
            mine[slot] = acc[t]

        @pl.when(who != me)
        def _(t=t, slot=slot):
            send[slot] = acc[t]

        counts[0] = counts[0] + (who == 0).astype(jnp.int32)
        counts[1] = counts[1] + (who != 0).astype(jnp.int32)

    def clear(out, used):
        def one(s, _):
            out[s] = jnp.zeros((BS, BS), F32)
            return 0

        lax.fori_loop(used, 32, one, 0)

    clear(mine, jnp.where(me == 0, counts[0], counts[1]))
    clear(send, jnp.where(me == 0, counts[1], counts[0]))


ANY = pl.BlockSpec(memory_space=pl.ANY)
SMEM = pl.BlockSpec(memory_space=pltpu.SMEM)
VMEM = pl.BlockSpec(memory_space=pltpu.VMEM)
HBM = pl.BlockSpec(memory_space=pltpu.HBM)
TILE = jax.ShapeDtypeStruct((32, BS, BS), F32)


def params(mebibytes):
    return pltpu.CompilerParams(vmem_limit_bytes=int(mebibytes * 2**20))


def cost(micros):
    return pl.CostEstimate(flops=0, bytes_accessed=int(micros * 3.6e6), transcendentals=0)


def packed(blocks, head=HDR):
    return jax.ShapeDtypeStruct((head + blocks * BS, BS), F32)


def multiply(micros, keep, held, parts, lows, halves, acc=None, left=None):
    number = len(parts)
    arrays = [part[j] for part in parts for j in halves]
    operands = [keep, held[1], held[0], *arrays]
    specs = [SMEM, SMEM, VMEM] + [HBM] * len(arrays)
    aliases = {}
    if acc is not None:
        aliases[len(operands)] = 0
        operands.append(acc)
        specs.append(VMEM)
    out_shape, out_specs = [TILE], [VMEM]
    scratch = [
        pltpu.VMEM((len(arrays) * GROUP + BS, BS), F32),
        pltpu.SMEM((-(-number // 2) * 8, BS), jnp.int32),
        pltpu.VMEM((number, HEADS, BS), F32),
        pltpu.VMEM((-(-number // 2) * 8, BS), jnp.int32),
        pltpu.SMEM((number * 4 * R_HALF * 4 + UNROLL,), jnp.int32),
        pltpu.SemaphoreType.DMA((len(arrays),)),
        pltpu.SemaphoreType.DMA((number,)),
        pltpu.SemaphoreType.DMA,
    ]
    if left is not None:
        aliases[2] = 1
        operands.append(left)
        specs.append(HBM)
        out_shape += [jax.ShapeDtypeStruct(array.shape, array.dtype) for array in held]
        out_specs += [VMEM, SMEM]
        scratch += [pltpu.SMEM((HDR, BS), F32), pltpu.SemaphoreType.DMA, pltpu.SemaphoreType.DMA]
    if len(halves) == 1:
        out_shape.append(jax.ShapeDtypeStruct((PLAN + 1,), jnp.int32))
        out_specs.append(SMEM)
    return pl.pallas_call(
        functools.partial(multiply_kernel, lows, halves, acc is None, left is not None),
        out_shape=out_shape,
        in_specs=specs,
        out_specs=out_specs,
        input_output_aliases=aliases,
        scratch_shapes=scratch,
        compiler_params=params(4 + 1.1 * len(arrays)),
        cost_estimate=cost(micros),
    )(*operands)


def finish(micros, plan, owner, held, parts, acc, flag):
    return pl.pallas_call(
        finish_kernel,
        out_shape=[TILE] * 3,
        in_specs=[SMEM, SMEM, VMEM, HBM, HBM, VMEM, VMEM],
        out_specs=[VMEM] * 3,
        input_output_aliases={5: 0},
        scratch_shapes=[pltpu.VMEM((2 * GROUP + BS, BS), F32), pltpu.SemaphoreType.DMA((2,))],
        compiler_params=params(6),
        cost_estimate=cost(micros),
    )(plan, owner, held[0], *parts, acc, flag)[1:]


def fence(arrays, after):
    shapes = [jax.ShapeDtypeStruct(array.shape, F32) for array in arrays]

    def nothing(*refs):
        pass

    return pl.pallas_call(
        nothing,
        out_shape=shapes,
        in_specs=[HBM] * len(arrays) + [ANY] * len(after),
        out_specs=[HBM] * len(arrays),
        input_output_aliases={i: i for i in range(len(arrays))},
        compiler_params=params(1),
    )(*arrays, *after)


def add_kernel(mine, other, out, total, sems):
    copies = []
    for i in range(4):
        rows = pl.ds(i * 8, 8)
        total[rows] = mine[rows] + other[rows]
        copies.append(pltpu.make_async_copy(total.at[rows], out.at[0, 0, rows], sems.at[i]))
        copies[-1].start()
    for copy in copies:
        copy.wait()


def add(mine, other):
    return pl.pallas_call(
        add_kernel,
        out_shape=jax.ShapeDtypeStruct((1, 1, 32, BS, BS), F32),
        in_specs=[VMEM, VMEM],
        out_specs=HBM,
        scratch_shapes=[pltpu.VMEM((32, BS, BS), F32), pltpu.SemaphoreType.DMA((4,))],
        compiler_params=params(8),
    )(mine, other)


def local(left_blocks, left_pattern, right_blocks, right_pattern, keep_mask, owner):
    early_a, early_b, late_a, late_b, packed_left = pl.pallas_call(
        pack_kernel,
        out_shape=[packed(R_PART)] * 2 + [packed(R_LATE, 0)] * 2 + [packed(L_CAP)],
        in_specs=[SMEM, SMEM, HBM, HBM],
        out_specs=[HBM] * 5,
        scratch_shapes=[
            pltpu.SMEM((33,), jnp.int32),
            pltpu.SMEM((65,), jnp.int32),
            pltpu.VMEM((2, HDR, BS), F32),
            pltpu.VMEM((HDR, BS), F32),
            pltpu.SemaphoreType.DMA((2 * R_HALF,)),
            pltpu.SemaphoreType.DMA((L_CAP,)),
            pltpu.SemaphoreType.DMA((3,)),
        ],
        compiler_params=params(1),
    )(left_pattern, right_pattern, left_blocks, right_blocks)
    early_a, early_b = hops(early_a, "x"), hops(early_b, "y")
    late_a, late_b = hops(late_a, "x"), hops(late_b, "y")
    lefts = hops(packed_left, "z", 1)
    (lefts[1],) = fence([lefts[1]], [early_a[3], early_b[3], late_a[3], late_b[3]])
    lefts.append(ring(lefts[1], "z"))
    array = jax.ShapeDtypeStruct((GROUP, BS), F32)
    merged = pl.pallas_call(
        merge_kernel,
        out_shape=[array] * 4,
        in_specs=[HBM] * 16,
        out_specs=[HBM] * 4,
        scratch_shapes=[
            pltpu.SMEM((2, 4, HDR, BS), F32),
            pltpu.SemaphoreType.DMA((8,)),
            pltpu.SemaphoreType.DMA((2, 2 * G_LATE)),
            pltpu.SemaphoreType.DMA((16,)),
        ],
        compiler_params=params(1),
        cost_estimate=cost(MERGE_COST),
    )(*early_a, *early_b, *late_a, *late_b)
    a0, b0 = hops(merged[0], "y", 2), hops(merged[2], "x", 2)
    a1, b1 = hops(merged[1], "y", 2), hops(merged[3], "x", 2)
    held = hold(lefts[0], 0)
    held = hold(lefts[1], 1, held)
    (lefts[2],) = fence([lefts[2]], [a0[1], b0[1], held[1]])
    lefts.append(ring(lefts[2], "z"))
    parts = [(a0[0], a1[0]), (b0[0], b1[0]), (a0[1], a1[1]), (b0[1], b1[1])]
    held = hold(lefts[2], 2, held)
    (acc,) = multiply(9, keep_mask, held, parts, (0,) * 4, (0, 1))
    a0[2], b0[2] = fence([a0[2], b0[2]], [acc])
    a0.append(ring(a0[2], "y"))
    b0.append(ring(b0[2], "x"))
    a1.append(ring(a1[2], "y"))
    b1.append(ring(b1[2], "x"))
    parts += [(a0[2], a1[2]), (b0[2], b1[2])]
    acc, *held = multiply(9, keep_mask, held, parts, (3,) * 4 + (0,) * 2, (0, 1), acc, lefts[3])
    flag = pl.pallas_call(
        flag_kernel,
        out_shape=jax.ShapeDtypeStruct((HDR, BS), F32),
        in_specs=[HBM] * 8 + [ANY],
        out_specs=VMEM,
        scratch_shapes=[pltpu.VMEM((8, HEADS, BS), F32), pltpu.SemaphoreType.DMA((8,))],
        compiler_params=params(1),
    )(*a0, *b0, acc)
    flag = functools.reduce(jnp.maximum, [flag] + [ring(flag, "z", distance) for distance in (1, 2, 3)])
    last = [(a0[3], a1[3]), (b0[3], b1[3])]
    acc, plan = multiply(5, keep_mask, held, last, (0, 0), (0,), acc)
    mine, send = finish(5, plan, owner.reshape(1, 1, 32), held, [a1[3], b1[3]], acc, flag)
    flag = jnp.maximum(flag, swap(flag))
    return lax.cond(
        flag[0, 0] > 0,
        lambda _: dense(left_blocks, left_pattern, right_blocks, right_pattern, keep_mask, owner)[None, None],
        lambda parts: add(*parts),
        (mine, swap(send)),
    )


def solution(mesh):
    return jax.shard_map(
        local,
        mesh=mesh,
        in_specs=(
            P("layer", "row", "col"),
            P("layer", "row", "col"),
            P("layer", "row", "col"),
            P("layer", "row", "col"),
            P("row", "col", None),
            P("row", "col", None, None),
        ),
        out_specs=P("row", "col", "layer", None, None),
        check_vma=False,
    )
```
